512 devices in a mesh: chrom: 256 (over x, z, y_lo, core), chan: 2 (over y_hi).
Axes of the slice: x: 4, y: 8 (y_hi: 2, y_lo: 4; y = y_hi * 4 + y_lo), z: 8, core: 2. Of those that a mesh axis runs over, the one named last changes fastest.
Arguments:
- embedding: bfloat16 [4096, 512], P('chrom'), may hold values from -6 to 6
- window_start: int32 [1], replicated, may hold values from 0 to 59999
- band_width: int32 [1], replicated, may hold values from 257 to 512
- dilations: int32 [2], replicated, may hold values from 1 to 8, as said below
- near_weight: bfloat16 [512, 48], P(None, 'chan'), may hold values from -0.25 to 0.25
- far_weight: bfloat16 [512, 48], P(None, 'chan'), may hold values from -0.25 to 0.25
- distance_bias: float32 [48, 512], P('chan'), may hold values from -3 to 3
- conv_weight: bfloat16 [2, 9, 48, 48], replicated, may hold values from -0.3125 to 0.3125
- conv_bias: float32 [2, 48], P(None, 'chan'), may hold values from -3 to 3
- cotangent: bfloat16 [48, 4096, 512], P('chan', 'chrom'), may hold values from -0.59765625 to 0.59765625
Outputs:
- pair_out: bfloat16 [48, 4096, 512], P('chan', 'chrom')
- embedding_grad: bfloat16 [4096, 512], P('chrom', 'chan')
The draws below stay inside these ranges and needn't reach their ends.
Inputs may be any that keep to these rules, and one draw needn't show every extreme that they name: Every entry of dilations is at least 1 and at most 8, and some layer's dilation equals 8.
All inputs are finite; a program needn't handle non-finite values.
Results may differ from the reference program's by a relative error of at most 0.0054.
Values may be sent and summed in bfloat16 or wider, within the bound.
No kernel may reach another device: no remote copies, remote signals or barrier semaphores. Data moves between devices by JAX's collectives and lax.ppermute only.
A program may use at most 64 MiB of HBM per device.

```python
import jax
import jax.numpy as jnp
from jax import lax

D = 512
C = 48
W = 512
R = 16
LAYERS = 2
DMAX = 8
NF = 16
BINS = 4096
N_CHROM = 256


def draw_dilations(key, part):
    key = jax.random.fold_in(key, 11)
    first_key, second_key = jax.random.split(key)
    spread = jax.random.randint(first_key, (LAYERS,), 1, DMAX + 1)
    largest = jax.random.randint(second_key, (), 0, LAYERS)
    layer_ids = jnp.arange(LAYERS, dtype=jnp.int32)
    return jnp.where(layer_ids == largest, DMAX, spread).astype(jnp.int32)


def block_levels(rng, extent, shards, least, top_value):
    factor_of = 1.0
    for dim, shards_of in shards:
        heights = jax.random.uniform(jax.random.fold_in(jax.random.fold_in(rng, 6), dim), (shards_of,), jnp.float32, least / len(shards), top_value / len(shards))
        factor_of = factor_of * jnp.repeat(jnp.exp(heights), extent[dim] // shards_of).reshape((-1,) + (1,) * (len(extent) - 1 - dim))
    return factor_of


def gaussian(key, extent, scale, reach, cuts=(), kind=jnp.bfloat16):
    factor_of = block_levels(key, extent, cuts, -0.22, 0.18) if cuts else 1.0
    values = jax.random.normal(key, extent, jnp.float32) * scale * factor_of
    return jnp.minimum(jnp.maximum(values, -reach), reach).astype(kind)


def setup_inputs(seed: int = 0) -> dict:
    keys = jax.random.split(jax.random.key(seed), 11)
    embedding = gaussian(keys[0], (BINS, D), 1.0, 6.0, ((0, 256),))
    window_start = jax.random.randint(keys[1], (1,), 0, 60000).astype(jnp.int32)
    band_width = jax.random.randint(keys[2], (1,), W // 2 + 1, W + 1).astype(jnp.int32)
    dilations = draw_dilations(jax.random.fold_in(keys[10], 71), 0)
    near_weight = gaussian(keys[4], (D, C), D ** -0.5, 0.25, ((1, 2),))
    far_weight = gaussian(keys[5], (D, C), D ** -0.5, 0.25, ((1, 2),))
    distance_bias = gaussian(keys[6], (C, W), 0.5, 3.0, ((0, 2),), jnp.float32)
    conv_weight = gaussian(keys[7], (LAYERS, 9, C, C), (9 * C) ** -0.5, 0.3125)
    conv_bias = gaussian(keys[8], (LAYERS, C), 0.5, 3.0, ((1, 2),), jnp.float32)
    cotangent = gaussian(keys[9], (C, BINS, W), 0.1, 0.59765625, ((0, 2), (1, 256)))
    return {"embedding": embedding, "window_start": window_start, "band_width": band_width, "dilations": dilations, "near_weight": near_weight, "far_weight": far_weight, "distance_bias": distance_bias, "conv_weight": conv_weight, "conv_bias": conv_bias, "cotangent": cotangent}


two_pi = 6.283185307179586

def gelu_exact(values):
    return jax.nn.gelu(values, approximate=False)

def wide_dot(left, right):
    return jnp.dot(left.astype(jnp.float32), right.astype(jnp.float32), precision=lax.Precision.HIGHEST)

def encode(row_ids, start_bin, feature_count):
    octave = jnp.arange(NF, dtype=jnp.int32)
    period = jnp.power(jnp.int32(2), octave + 2).astype(jnp.int32)
    residue = jnp.remainder(start_bin + row_ids[:, None], period[None, :]).astype(jnp.int32)
    angles = residue.astype(jnp.float32) * (two_pi / period.astype(jnp.float32))[None, :]
    encoding = jnp.concatenate((jnp.sin(angles), jnp.cos(angles)), axis=1)
    return jnp.pad(encoding, ((0, 0), (0, feature_count - 2 * NF)))

def band_mask(row_ids, width_value, total_rows):
    offsets = jnp.arange(W, dtype=jnp.int32)
    inside = (offsets[None, :] < width_value) & (row_ids[:, None] + offsets[None, :] < total_rows)
    return inside.astype(jnp.float32)

def convolve(active, kernel, dilation, sign):
    padded = jnp.pad(active, ((0, 0), (DMAX, DMAX), (2 * DMAX, 2 * DMAX)))
    kernel_wide = kernel.astype(jnp.float32)

    def row_block(block_id):
        base = block_id * R
        running = jnp.zeros((C, R * W), jnp.float32)
        for tap_index in range(9):
            row_step = tap_index // 3 - 1
            col_step = tap_index % 3 - 1
            row_start = (base + DMAX + sign * row_step * dilation).astype(jnp.int32)
            col_start = (2 * DMAX + sign * (col_step - row_step) * dilation).astype(jnp.int32)
            tap_slice = lax.dynamic_slice(padded, (jnp.int32(0), row_start, col_start), (C, R, W))
            running = running + jnp.dot(kernel_wide[tap_index], tap_slice.astype(jnp.float32).reshape(C, R * W), precision=lax.Precision.HIGHEST)
        return running.reshape(C, R, W)
    blocks = lax.map(row_block, jnp.arange(N_CHROM, dtype=jnp.int32))
    return jnp.transpose(blocks, (1, 0, 2, 3)).reshape(C, BINS, W)

def reference(embedding, window_start, band_width, dilations, near_weight, far_weight, distance_bias, conv_weight, conv_bias, cotangent):
    row_ids = jnp.arange(BINS, dtype=jnp.int32)
    band_keep = band_mask(row_ids, band_width[0], BINS)
    features = (embedding.astype(jnp.float32) + encode(row_ids, window_start[0], D)).astype(jnp.bfloat16)
    near_proj = wide_dot(features, near_weight).T
    far_proj = wide_dot(features, far_weight).T
    far_padded = jnp.pad(far_proj, ((0, 0), (0, W)))
    local_lookup = (jnp.arange(R, dtype=jnp.int32)[:, None] + jnp.arange(W, dtype=jnp.int32)[None, :]).astype(jnp.int32)

    def ahead_block(block_id):
        base = (block_id * R).astype(jnp.int32)
        piece = lax.dynamic_slice(far_padded, (jnp.int32(0), base), (C, R + W))
        return piece[:, local_lookup]
    ahead_blocks = lax.map(ahead_block, jnp.arange(N_CHROM, dtype=jnp.int32))
    ahead = jnp.transpose(ahead_blocks, (1, 0, 2, 3)).reshape(C, BINS, W)
    pair_state = band_keep[None] * (near_proj[:, :, None] + ahead + distance_bias[:, None, :])
    states = []
    for layer_idx in range(LAYERS):
        states.append(pair_state)
        active = gelu_exact(pair_state).astype(jnp.bfloat16)
        conv_out = convolve(active, conv_weight[layer_idx], dilations[layer_idx], 1)
        pair_state = band_keep[None] * (pair_state + conv_out + conv_bias[layer_idx][:, None, None])
    pair_out = pair_state.astype(jnp.bfloat16)
    pair_grad = band_keep[None] * cotangent.astype(jnp.float32)
    for layer_idx in reversed(range(LAYERS)):
        back_conv = convolve(pair_grad.astype(jnp.bfloat16), jnp.swapaxes(conv_weight[layer_idx], 1, 2), dilations[layer_idx], -1)
        slope_term = jax.vjp(gelu_exact, states[layer_idx])[1](back_conv)[0]
        pair_grad = band_keep[None] * (pair_grad + slope_term)
    grad_near = lax.optimization_barrier(jnp.sum(pair_grad, axis=2))

    def add_diagonal(offset, running):
        offset = offset.astype(jnp.int32)
        column = lax.dynamic_slice_in_dim(pair_grad, offset, 1, 2)[:, :, 0]
        padded_col = jnp.pad(column, ((0, 0), (W, 0)))
        return running + lax.dynamic_slice_in_dim(padded_col, (W - offset).astype(jnp.int32), BINS, 1)
    grad_far = lax.fori_loop(0, W, add_diagonal, jnp.zeros((C, BINS), jnp.float32))
    near_low = grad_near.astype(jnp.bfloat16).T
    far_low = grad_far.astype(jnp.bfloat16).T
    embedding_grad = wide_dot(near_low, near_weight.T) + wide_dot(far_low, far_weight.T)
    return (pair_out, embedding_grad.astype(jnp.bfloat16))
```

```python
import functools

import jax
import jax.numpy as jnp
from jax import lax
from jax.experimental import pallas as pl
from jax.experimental.pallas import tpu as pltpu
from jax.sharding import PartitionSpec as P

DMAX = 8
NF = 16
HALO = 2 * DMAX
LANES = 128
SHIFTS = (-2, -1, 0, 1, 2)

two_pi = 6.283185307179586
inv_sqrt2 = 0.7071067811865476
inv_sqrt_2pi = 0.3989422804014327


def encode(row_ids, start_bin, feature_count):
    octave = jnp.arange(NF, dtype=jnp.int32)
    period = jnp.power(jnp.int32(2), octave + 2).astype(jnp.int32)
    residue = jnp.remainder(start_bin + row_ids[:, None], period[None, :])
    angles = residue.astype(jnp.float32) * (two_pi / period.astype(jnp.float32))[None, :]
    encoding = jnp.concatenate((jnp.sin(angles), jnp.cos(angles)), axis=1)
    return jnp.pad(encoding, ((0, 0), (0, feature_count - 2 * NF)))


def from_ahead(block, distance):
    devices = range(lax.axis_size("chrom"))
    route = [(i + distance, i) for i in devices if i + distance in devices]
    return lax.ppermute(block, "chrom", route)


def from_partner(block):
    return lax.ppermute(block, "chan", [(0, 1), (1, 0)])


def diagonal_from_behind(block):
    count = lax.axis_size("chrom")
    route = [(2 * (i - 1) + 1 - c, 2 * i + c) for i in range(1, count) for c in range(2)]
    return lax.ppermute(block, ("chrom", "chan"), route)


def stacked_taps(kernel, sign, out_count):
    chan_count = kernel.shape[1]
    rows = []
    for m in SHIFTS:
        blocks = []
        for a in (-1, 0, 1):
            b = a + m
            if -1 <= b <= 1:
                tap = kernel[3 * (sign * a + 1) + sign * b + 1]
                blocks.append((tap if sign > 0 else tap.T)[:out_count])
            else:
                blocks.append(jnp.zeros((out_count, chan_count), kernel.dtype))
        rows.append(jnp.concatenate(blocks, axis=1))
    return jnp.concatenate(rows, axis=0)


def lane_ids():
    return lax.broadcasted_iota(jnp.int32, (1, LANES), 1)


def tiles_of(values):
    return [values[:, k : k + LANES] for k in range(0, values.shape[1], LANES)]


def pull(tiles, amount, count, lanes):
    turned = [pltpu.roll(tile, lax.rem(LANES - amount, LANES), 1) for tile in tiles]
    turned.append(jnp.zeros_like(turned[0]))
    inside = lanes < LANES - amount
    return [jnp.where(inside, turned[k], turned[k + 1]) for k in range(count)]


def push(tiles, amount, count, lanes):
    zero = jnp.zeros_like(tiles[0])
    turned = [zero] + [pltpu.roll(tile, amount, 1) for tile in tiles] + [zero]
    inside = lanes >= amount
    return [jnp.where(inside, turned[k + 1], turned[k]) for k in range(count)]


def tap_sum(weights, window, out_count, dilation, lanes):
    stacked = jnp.dot(weights, window, preferred_element_type=jnp.float32)
    part = [tiles_of(stacked[k * out_count : (k + 1) * out_count]) for k in range(5)]
    count = len(part[0])
    shifted = [
        push(part[0], 2 * dilation, count, lanes),
        push(part[1], dilation, count, lanes),
        part[2],
        pull(part[3], dilation, count, lanes),
        pull(part[4], 2 * dilation, count, lanes),
    ]
    return [sum(tile[1:], tile[0]) for tile in zip(*shifted)]


def three_rows(ref, row, dilation):
    return jnp.concatenate((ref[row - dilation], ref[row], ref[row + dilation]), axis=0)


def limit_of(row, first_row, band_width, total_rows):
    here = first_row - HALO + row
    return jnp.where(here < 0, 0, jnp.minimum(band_width, total_rows - here))


def gelu_cdf(values):
    return 0.5 + 0.5 * lax.erf(values * inv_sqrt2)


def gelu_slope(values, cdf):
    return cdf + values * (inv_sqrt_2pi * jnp.exp(-0.5 * values * values))


def forward_kernel(
    total_rows, scalars, near, far, bias, bias_0, bias_1, taps_0, taps_1,
    pair_out, slope_0, slope_1, pair_0, act_0, act_1, pair_1,
):
    band_width, first_row, step_0, step_1 = (scalars[k] for k in range(4))
    lanes = lane_ids()
    own = pair_out.shape[1]
    width = bias.shape[1]
    count = width // LANES
    rows = pair_out.shape[0]

    def keeps(row):
        limit = limit_of(row, first_row, band_width, total_rows)
        return [lanes + k * LANES < limit for k in range(count)]

    def seed(row, with_slope):
        near_col = pltpu.roll(near[...], lax.rem(LANES - row, LANES), 1)[:, 0:1]
        ahead = pull(tiles_of(far[...]), row, count, lanes)
        for k, keep in enumerate(keeps(row)):
            span = pl.ds(k * LANES, LANES)
            value = jnp.where(keep, near_col + ahead[k] + bias[:, span], 0.0)
            cdf = gelu_cdf(value)
            pair_0[row, :, span] = value
            act_0[row, :, span] = (value * cdf).astype(jnp.bfloat16)
            if with_slope:
                slope_0[row - HALO, :, span] = gelu_slope(value[:own], cdf[:own])

    def outer_seed(index, _):
        seed(jnp.where(index < HALO, index, index + rows), False)
        return 0

    def inner_seed(index, _):
        seed(index + HALO, True)
        return 0

    lax.fori_loop(0, 2 * HALO, outer_seed, 0)
    lax.fori_loop(0, rows, inner_seed, 0)

    def layer_0(index, _):
        row = index + DMAX
        conv = tap_sum(taps_0[...], three_rows(act_0, row, step_0), near.shape[0], step_0, lanes)
        for k, keep in enumerate(keeps(row)):
            span = pl.ds(k * LANES, LANES)
            value = jnp.where(keep, pair_0[row, :, span] + conv[k] + bias_0[...], 0.0)
            cdf = gelu_cdf(value)
            pair_1[index, :, span] = value[:own]
            act_1[index, :, span] = (value * cdf).astype(jnp.bfloat16)
            slope_1[index, :, span] = gelu_slope(value, cdf)
        return 0

    lax.fori_loop(0, rows + HALO, layer_0, 0)

    def layer_1(index, _):
        row = index + HALO
        conv = tap_sum(taps_1[...], three_rows(act_1, row - DMAX, step_1), own, step_1, lanes)
        for k, keep in enumerate(keeps(row)):
            span = pl.ds(k * LANES, LANES)
            value = jnp.where(keep, pair_1[row - DMAX, :, span] + conv[k] + bias_1[...], 0.0)
            pair_out[index, :, span] = value
        return 0

    lax.fori_loop(0, rows, layer_1, 0)


def backward_kernel(
    total_rows, scalars, cot_behind, cot_here, cot_ahead, slope_0, slope_1, taps_1, taps_0,
    near_sum, far_sum, grad_2, grad_1, low_1,
):
    band_width, first_row, step_0, step_1 = (scalars[k] for k in range(4))
    lanes = lane_ids()
    rows, chans, width = cot_here.shape
    own = slope_0.shape[1]
    count = width // LANES

    def keeps(row):
        limit = limit_of(row, first_row, band_width, total_rows)
        return [lanes + k * LANES < limit for k in range(count)]

    def lay(index, _):
        grad_2[index] = cot_behind[index]
        grad_2[index + rows] = cot_here[index]
        grad_2[index + 2 * rows] = cot_ahead[index]
        return 0

    lax.fori_loop(0, rows, lay, 0)

    def layer_1(index, _):
        row = index + DMAX
        conv = tap_sum(taps_1[...], three_rows(grad_2, row, step_1), chans, step_1, lanes)
        for k, keep in enumerate(keeps(row)):
            span = pl.ds(k * LANES, LANES)
            above = grad_2[row, :, span].astype(jnp.float32)
            value = jnp.where(keep, above + slope_1[index, :, span] * conv[k], 0.0)
            grad_1[index, :, span] = value[:own]
            low_1[index, :, span] = value.astype(jnp.bfloat16)
        return 0

    lax.fori_loop(0, rows + HALO, layer_1, 0)

    near_sum[...] = jnp.zeros_like(near_sum)
    far_sum[...] = jnp.zeros_like(far_sum)

    def layer_0(index, _):
        row = index + HALO
        conv = tap_sum(taps_0[...], three_rows(low_1, row - DMAX, step_0), own, step_0, lanes)
        values = []
        for k, keep in enumerate(keeps(row)):
            span = pl.ds(k * LANES, LANES)
            values.append(
                jnp.where(keep, grad_1[row - DMAX, :, span] + slope_0[index, :, span] * conv[k], 0.0)
            )
        total = jnp.sum(sum(values[1:], values[0]), axis=1, keepdims=True)
        near_sum[...] += jnp.where(lanes == index, total, 0.0)
        for k, tile in enumerate(push(values, index, count + 1, lanes)):
            far_sum[:, k * LANES : (k + 1) * LANES] += tile
        return 0

    lax.fori_loop(0, rows, layer_0, 0)


def call(kernel, out_shapes, scratch, flops, smem, *arrays):
    bytes_accessed = sum(a.size * a.dtype.itemsize for a in arrays)
    bytes_accessed += sum(s.size * s.dtype.itemsize for s in out_shapes)
    vmem = pl.BlockSpec(memory_space=pltpu.VMEM)
    return pl.pallas_call(
        kernel,
        out_shape=out_shapes,
        in_specs=[pl.BlockSpec(memory_space=pltpu.SMEM)] + [vmem] * len(arrays),
        out_specs=[vmem] * len(out_shapes),
        scratch_shapes=scratch,
        compiler_params=pltpu.CompilerParams(vmem_limit_bytes=40 * 2**20),
        cost_estimate=pl.CostEstimate(
            flops=flops, bytes_accessed=bytes_accessed, transcendentals=0
        ),
    )(smem, *arrays)


def gather_band(far, distance_blocks, rows_here):
    behind = from_ahead(far, -1)
    held = jnp.concatenate((far, from_ahead(far, 1)), axis=0)
    beyond = from_ahead(held, distance_blocks)
    step = 2
    while step < distance_blocks:
        held = jnp.concatenate((held, from_ahead(held, step)), axis=0)
        step *= 2
    return jnp.concatenate((behind, held, beyond), axis=0)


def return_band(partial, distance_blocks, rows_here):
    last = partial[distance_blocks * rows_here :]
    held = partial[: distance_blocks * rows_here]
    from_last = from_ahead(last, -distance_blocks)
    step = distance_blocks // 2
    while step > 1:
        cut = step * rows_here
        held = held[:cut] + from_ahead(held[cut:], -step)
        step //= 2
    return held[:rows_here] + from_last, held[rows_here:]


def shards(
    embedding, window_start, band_width, dilations, near_weight, far_weight,
    distance_bias, conv_weight, conv_bias, cotangent,
):
    rows = embedding.shape[0]
    own, width = distance_bias.shape
    blocks = width // rows
    chans = conv_weight.shape[2]
    features_half = embedding.shape[1] // 2
    chan = lax.axis_index("chan")
    first_row = lax.axis_index("chrom") * rows
    total_rows = lax.axis_size("chrom") * rows
    row_ids = first_row + jnp.arange(rows, dtype=jnp.int32)
    scalars = jnp.stack([band_width[0], first_row, dilations[0], dilations[1]]).astype(jnp.int32)

    cot_other = from_partner(cotangent)

    features = (
        embedding.astype(jnp.float32) + encode(row_ids, window_start[0], embedding.shape[1])
    ).astype(jnp.bfloat16)
    both = jnp.concatenate((near_weight, far_weight), axis=1)
    proj = jnp.dot(features, both, preferred_element_type=jnp.float32)
    proj_other = from_partner(proj)
    near = jnp.concatenate((proj[:, :own], proj_other[:, :own]), axis=1)
    far = jnp.concatenate((proj[:, own:], proj_other[:, own:]), axis=1)
    near_band = jnp.concatenate((from_ahead(near, -1), near, from_ahead(near, 1)), axis=0)
    far_band = gather_band(far, blocks, rows)
    near_t = jnp.pad(near_band.T, ((0, 0), (0, LANES - 3 * rows)))
    far_t = jnp.pad(far_band.T, ((0, 0), (0, width + LANES - far_band.shape[0])))

    small = jnp.concatenate((distance_bias, conv_bias.T, jnp.zeros((own, LANES - 2), jnp.float32)), axis=1)
    small = jnp.concatenate((small, from_partner(small)), axis=0)
    bias = small[:, :width]
    both_other = from_partner(lax.dynamic_slice_in_dim(both, (1 - chan) * features_half, features_half, 0))
    both_here = lax.dynamic_slice_in_dim(both, chan * features_half, features_half, 0)
    near_cols = jnp.concatenate((both_here[:, :own], both_other[:, :own]), axis=1)
    far_cols = jnp.concatenate((both_here[:, own:], both_other[:, own:]), axis=1)

    twice = jnp.concatenate((conv_weight, conv_weight), axis=2)
    twice = jnp.concatenate((twice, twice), axis=3)
    turned = lax.dynamic_slice(
        twice, (0, 0, chan * own, chan * own), conv_weight.shape
    )
    pad_rows = lambda taps: jnp.pad(taps, ((0, -taps.shape[0] % 16), (0, 0)))
    ahead_0 = stacked_taps(turned[0], 1, chans)
    ahead_1 = pad_rows(stacked_taps(turned[1], 1, own))
    back_1 = stacked_taps(turned[1], -1, chans)
    back_0 = pad_rows(stacked_taps(turned[0], -1, own))

    per_row = 2 * 15 * chans * chans * width
    f32 = functools.partial(jax.ShapeDtypeStruct, dtype=jnp.float32)
    pair_rows, slope_0, slope_1 = call(
        functools.partial(forward_kernel, total_rows),
        (f32((rows, own, width)), f32((rows, own, width)), f32((rows + HALO, chans, width))),
        [
            pltpu.VMEM((rows + 2 * HALO, chans, width), jnp.float32),
            pltpu.VMEM((rows + 2 * HALO, chans, width), jnp.bfloat16),
            pltpu.VMEM((rows + HALO, chans, width), jnp.bfloat16),
            pltpu.VMEM((rows + HALO, own, width), jnp.float32),
        ],
        per_row * 40,
        scalars, near_t, far_t, bias, small[:, width : width + 1], small[:own, width + 1 : width + 2],
        ahead_0, ahead_1,
    )
    pair_out = jnp.swapaxes(pair_rows.astype(jnp.bfloat16), 0, 1)

    offsets = jnp.arange(width, dtype=jnp.int32)
    keep = (offsets[None, :] < band_width[0]) & (row_ids[:, None] + offsets[None, :] < total_rows)
    cot = jnp.concatenate((cotangent, cot_other), axis=0)
    cot = jnp.where(keep[:, None, :], jnp.swapaxes(cot, 0, 1), 0).astype(jnp.bfloat16)
    cot_behind = from_ahead(cot, -1)
    cot_ahead = from_ahead(cot, 1)
    near_sum, far_sum = call(
        functools.partial(backward_kernel, total_rows),
        (f32((own, LANES)), f32((own, width + LANES))),
        [
            pltpu.VMEM((rows + 2 * HALO, chans, width), jnp.bfloat16),
            pltpu.VMEM((rows + HALO, own, width), jnp.float32),
            pltpu.VMEM((rows + HALO, chans, width), jnp.bfloat16),
        ],
        per_row * 40,
        scalars, cot_behind, cot, cot_ahead, slope_0, slope_1, back_1, back_0,
    )
    far_terms = far_sum[:, : width + rows].T
    grad_near = near_sum[:, :rows].T
    here, onward = return_band(far_terms, blocks, rows)
    near_here = jnp.concatenate((here, grad_near), axis=1)
    other = from_partner(near_here)
    grad_far = here + from_ahead(onward, -1)
    grad_far_other = other[:, :own] + diagonal_from_behind(onward)
    near_low = jnp.concatenate((grad_near, other[:, own:]), axis=1).astype(jnp.bfloat16)
    far_low = jnp.concatenate((grad_far, grad_far_other), axis=1).astype(jnp.bfloat16)
    lows = jnp.concatenate((near_low, far_low), axis=1)
    cols = jnp.concatenate((near_cols, far_cols), axis=1)
    embedding_grad = lax.dot_general(
        lows, cols, (((1,), (1,)), ((), ())), preferred_element_type=jnp.float32
    ).astype(jnp.bfloat16)
    return (pair_out, embedding_grad)


def solution(mesh):
    in_specs = (
        P("chrom", None),
        P(),
        P(),
        P(),
        P(None, "chan"),
        P(None, "chan"),
        P("chan", None),
        P(),
        P(None, "chan"),
        P("chan", "chrom", None),
    )
    out_specs = (P("chan", "chrom", None), P("chrom", "chan"))
    return jax.shard_map(shards, mesh=mesh, in_specs=in_specs, out_specs=out_specs, check_vma=False)
```

```python
import functools

import jax
import jax.numpy as jnp
from jax import lax
from jax.experimental import pallas as pl
from jax.experimental.pallas import tpu as pltpu
from jax.sharding import PartitionSpec as P

DMAX = 8
NF = 16
HALO = 2 * DMAX
LANES = 128
SPARE = 32
SHIFTS = (-2, -1, 0, 1, 2)
GROUP = 8

two_pi = 6.283185307179586
inv_sqrt2 = 0.7071067811865476
inv_sqrt_2pi = 0.3989422804014327


def encode(row_ids, start_bin, feature_count):
    octave = jnp.arange(NF, dtype=jnp.int32)
    period = jnp.power(jnp.int32(2), octave + 2).astype(jnp.int32)
    residue = jnp.remainder(start_bin + row_ids[:, None], period[None, :])
    angles = residue.astype(jnp.float32) * (two_pi / period.astype(jnp.float32))[None, :]
    encoding = jnp.concatenate((jnp.sin(angles), jnp.cos(angles)), axis=1)
    return jnp.pad(encoding, ((0, 0), (0, feature_count - 2 * NF)))


def from_ahead(block, distance):
    devices = range(lax.axis_size("chrom"))
    route = [(i + distance, i) for i in devices if i + distance in devices]
    return lax.ppermute(block, "chrom", route)


def from_partner(block):
    return lax.ppermute(block, "chan", [(0, 1), (1, 0)])


def stacked_taps(kernel, sign, out_count):
    chan_count = kernel.shape[1]
    rows = []
    for m in SHIFTS:
        blocks = []
        for a in (-1, 0, 1):
            b = a + m
            if -1 <= b <= 1:
                tap = kernel[3 * (sign * a + 1) + sign * b + 1]
                blocks.append((tap if sign > 0 else tap.T)[:out_count])
            else:
                blocks.append(jnp.zeros((out_count, chan_count), kernel.dtype))
        rows.append(jnp.concatenate(blocks, axis=1))
    return jnp.concatenate(rows, axis=0)


def lane_ids():
    return lax.broadcasted_iota(jnp.int32, (1, LANES), 1)


def tiles_of(values):
    return [values[:, k : k + LANES] for k in range(0, values.shape[1], LANES)]


def pull(tiles, amount, count, lanes):
    turned = [pltpu.roll(tile, lax.rem(LANES - amount, LANES), 1) for tile in tiles]
    turned.append(jnp.zeros_like(turned[0]))
    inside = lanes < LANES - amount
    return [jnp.where(inside, turned[k], turned[k + 1]) for k in range(count)]


def push(tiles, amount, count, lanes):
    zero = jnp.zeros_like(tiles[0])
    turned = [zero] + [pltpu.roll(tile, amount, 1) for tile in tiles] + [zero]
    inside = lanes >= amount
    return [jnp.where(inside, turned[k + 1], turned[k]) for k in range(count)]


def tap_sums(weights, ref, first, dilation, out_count, lanes):
    width = ref.shape[2]
    count = width // LANES
    window = jnp.concatenate(
        [
            jnp.concatenate([ref[first + g + a * dilation] for a in (-1, 0, 1)], axis=0)
            for g in range(GROUP)
        ],
        axis=1,
    )
    stacked = jnp.dot(weights[...], window, preferred_element_type=jnp.float32)
    sums = []
    for g in range(GROUP):
        part = [
            tiles_of(stacked[k * out_count : (k + 1) * out_count, g * width : (g + 1) * width])
            for k in range(5)
        ]
        shifted = [
            push(part[0], 2 * dilation, count, lanes),
            push(part[1], dilation, count, lanes),
            part[2],
            pull(part[3], dilation, count, lanes),
            pull(part[4], 2 * dilation, count, lanes),
        ]
        sums.append([sum(tile[1:], tile[0]) for tile in zip(*shifted)])
    return sums


def limit_of(row, first_row, band_width, total_rows):
    here = first_row - HALO + row
    return jnp.where(here < 0, 0, jnp.minimum(band_width, total_rows - here))


def gelu_cdf(values):
    return 0.5 + 0.5 * lax.erf(values * inv_sqrt2)


def gelu_slope(values, cdf):
    return cdf + values * (inv_sqrt_2pi * jnp.exp(-0.5 * values * values))


def forward_kernel(
    total_rows, scalars, terms, params, taps,
    pair_out, slope_0, slope_1, pair_0, act_0, act_1, pair_1, far_rows, near_rows, far, near,
):
    band_width, first_row, step_0, step_1, member = (scalars[k] for k in range(5))
    lanes = lane_ids()
    rows, own, width = pair_out.shape
    chans = 2 * own
    count = width // LANES
    members = terms.shape[0]
    taps_0, taps_1 = taps.at[: 5 * chans], taps.at[5 * chans :]
    bias = params.at[:, :width]
    bias_0 = params[:, width : width + LANES][:, 0:1]
    bias_1 = params[:own, width : width + LANES][:, 1:2]

    far_rows[...] = jnp.zeros_like(far_rows)
    near_rows[...] = jnp.zeros_like(near_rows)
    half = rows // 2
    for place in range(width // rows + 3):
        source = lax.rem(member + (members - 1 + place), members)
        tile = terms[source, place // members]
        far_rows[place * rows : place * rows + half] = tile
        far_rows[place * rows + half : (place + 1) * rows] = pltpu.roll(tile, LANES - chans, 1)
        if place < 3:
            tile = jnp.zeros((half, LANES), jnp.float32)
            for j in range(3):
                part = pltpu.roll(terms[source, j], SPARE * (j + 1), 1)
                tile = jnp.where(lanes // SPARE == j, part, tile)
            near_rows[place * rows : place * rows + half] = tile
            near_rows[place * rows + half : (place + 1) * rows] = pltpu.roll(tile, LANES - chans, 1)
    for k in range(count + 1):
        span = slice(k * LANES, (k + 1) * LANES)
        far[:, span] = far_rows[span].T[:chans]
    near[...] = near_rows[...].T[:chans]

    def keeps(row):
        limit = limit_of(row, first_row, band_width, total_rows)
        return [lanes + k * LANES < limit for k in range(count)]

    def seed(row, with_slope):
        near_col = pltpu.roll(near[...], lax.rem(LANES - row, LANES), 1)[:, 0:1]
        ahead = pull(tiles_of(far[...]), row, count, lanes)
        for k, keep in enumerate(keeps(row)):
            span = pl.ds(k * LANES, LANES)
            value = jnp.where(keep, near_col + ahead[k] + bias[:, span], 0.0)
            cdf = gelu_cdf(value)
            pair_0[row, :, span] = value
            act_0[row, :, span] = (value * cdf).astype(jnp.bfloat16)
            if with_slope:
                slope_0[row - HALO, :, span] = gelu_slope(value[:own], cdf[:own])

    def outer_seed(index, _):
        seed(jnp.where(index < HALO, index, index + rows), False)
        return 0

    def inner_seed(index, _):
        seed(index + HALO, True)
        return 0

    lax.fori_loop(0, 2 * HALO, outer_seed, 0)
    lax.fori_loop(0, rows, inner_seed, 0)

    def layer_0(block, _):
        first = block * GROUP
        convs = tap_sums(taps_0, act_0, first + DMAX, step_0, chans, lanes)
        for g, conv in enumerate(convs):
            index = first + g
            row = index + DMAX
            for k, keep in enumerate(keeps(row)):
                span = pl.ds(k * LANES, LANES)
                value = jnp.where(keep, pair_0[row, :, span] + conv[k] + bias_0, 0.0)
                cdf = gelu_cdf(value)
                pair_1[index, :, span] = value[:own]
                act_1[index, :, span] = (value * cdf).astype(jnp.bfloat16)
                slope_1[index, :, span] = gelu_slope(value, cdf)
        return 0

    lax.fori_loop(0, (rows + HALO) // GROUP, layer_0, 0)

    def layer_1(block, _):
        first = block * GROUP
        convs = tap_sums(taps_1, act_1, first + DMAX, step_1, own, lanes)
        for g, conv in enumerate(convs):
            index = first + g
            for k, keep in enumerate(keeps(index + HALO)):
                span = pl.ds(k * LANES, LANES)
                value = jnp.where(keep, pair_1[index + DMAX, :, span] + conv[k] + bias_1, 0.0)
                pair_out[index, :, span] = value
        return 0

    lax.fori_loop(0, rows // GROUP, layer_1, 0)


def backward_kernel(
    total_rows, scalars, cot_behind, cot_here, cot_ahead, slope_0, slope_1, taps,
    far_terms, near_terms, grad_2, grad_1, low_1, near_sum, far_sum, far_rows,
):
    band_width, first_row, step_0, step_1, member = (scalars[k] for k in range(5))
    lanes = lane_ids()
    rows, chans, width = cot_here.shape
    own = chans // 2
    count = width // LANES
    members = far_terms.shape[0]
    taps_1, taps_0 = taps.at[: 5 * chans], taps.at[5 * chans :]

    def keeps(row):
        limit = limit_of(row, first_row, band_width, total_rows)
        return [lanes + k * LANES < limit for k in range(count)]

    def lay(index, _):
        grad_2[index] = cot_behind[index]
        grad_2[index + rows] = cot_here[index]
        grad_2[index + 2 * rows] = cot_ahead[index]
        return 0

    lax.fori_loop(0, rows, lay, 0)

    def layer_1(block, _):
        first = block * GROUP
        convs = tap_sums(taps_1, grad_2, first + DMAX, step_1, chans, lanes)
        for g, conv in enumerate(convs):
            index = first + g
            row = index + DMAX
            for k, keep in enumerate(keeps(row)):
                span = pl.ds(k * LANES, LANES)
                above = grad_2[row, :, span].astype(jnp.float32)
                value = jnp.where(keep, above + slope_1[index, :, span] * conv[k], 0.0)
                grad_1[index, :, span] = value[:own]
                low_1[index, :, span] = value.astype(jnp.bfloat16)
        return 0

    lax.fori_loop(0, (rows + HALO) // GROUP, layer_1, 0)

    near_sum[...] = jnp.zeros_like(near_sum)
    far_sum[...] = jnp.zeros_like(far_sum)

    def layer_0(block, _):
        first = block * GROUP
        convs = tap_sums(taps_0, low_1, first + DMAX, step_0, own, lanes)
        for g, conv in enumerate(convs):
            index = first + g
            values = []
            for k, keep in enumerate(keeps(index + HALO)):
                span = pl.ds(k * LANES, LANES)
                above = grad_1[index + DMAX, :, span]
                values.append(jnp.where(keep, above + slope_0[index, :, span] * conv[k], 0.0))
            total = jnp.sum(sum(values[1:], values[0]), axis=1, keepdims=True)
            near_sum[:own] += jnp.where(lanes == index, total, 0.0)
            for k, tile in enumerate(push(values, index, count + 1, lanes)):
                far_sum[:own, k * LANES : (k + 1) * LANES] += tile
        return 0

    lax.fori_loop(0, rows // GROUP, layer_0, 0)

    far_rows[...] = jnp.zeros_like(far_rows)
    for k in range(count + 1):
        start = pl.multiple_of(member * rows, 8) + k * LANES
        far_rows[pl.ds(start, LANES)] = far_sum[:, k * LANES : (k + 1) * LANES].T
    half = rows // 2

    def halves(slot):
        return [far_rows[slot * rows + h * half : slot * rows + (h + 1) * half] for h in range(2)]

    for r in range(members):
        pieces = halves(r) + halves(members + r)
        far_terms[r, 0] = sum(
            [pltpu.roll(piece, k * own, 1) for k, piece in enumerate(pieces) if k], pieces[0]
        )
        pieces = halves(2 * members + r)
        far_terms[r, 1] = pieces[0] + pltpu.roll(pieces[1], own, 1)
    near_rows = near_sum[...].T
    near_terms[...] = pltpu.roll(near_rows[:half], 2 * own, 1) + pltpu.roll(
        near_rows[half:rows], 3 * own, 1
    )


def call(kernel, out_shapes, scratch, flops, smem, *arrays):
    bytes_accessed = sum(a.size * a.dtype.itemsize for a in arrays)
    bytes_accessed += sum(s.size * s.dtype.itemsize for s in out_shapes)
    vmem = pl.BlockSpec(memory_space=pltpu.VMEM)
    return pl.pallas_call(
        kernel,
        out_shape=out_shapes,
        in_specs=[pl.BlockSpec(memory_space=pltpu.SMEM)] + [vmem] * len(arrays),
        out_specs=[vmem] * len(out_shapes),
        scratch_shapes=scratch,
        compiler_params=pltpu.CompilerParams(vmem_limit_bytes=32 * 2**20),
        cost_estimate=pl.CostEstimate(
            flops=flops, bytes_accessed=bytes_accessed, transcendentals=0
        ),
    )(smem, *arrays)


def forward_call(total_rows, rows, scalars, terms, params, taps):
    chans, width = params.shape[0], params.shape[1] - LANES
    own = chans // 2
    f32 = functools.partial(jax.ShapeDtypeStruct, dtype=jnp.float32)
    return call(
        functools.partial(forward_kernel, total_rows),
        (f32((rows, own, width)), f32((rows, own, width)), f32((rows + HALO, chans, width))),
        [
            pltpu.VMEM((rows + 2 * HALO, chans, width), jnp.float32),
            pltpu.VMEM((rows + 2 * HALO, chans, width), jnp.bfloat16),
            pltpu.VMEM((rows + HALO, chans, width), jnp.bfloat16),
            pltpu.VMEM((rows + HALO, own, width), jnp.float32),
            pltpu.VMEM((width + LANES, LANES), jnp.float32),
            pltpu.VMEM((LANES, LANES), jnp.float32),
            pltpu.VMEM((chans, width + LANES), jnp.float32),
            pltpu.VMEM((chans, LANES), jnp.float32),
        ],
        2 * 15 * chans * chans * width * 40,
        scalars, terms, params, taps,
    )


def backward_call(total_rows, members, scalars, cot_behind, cot, cot_ahead, slope_0, slope_1, taps):
    rows, chans, width = cot.shape
    own = chans // 2
    slots = members + (width + LANES) // rows
    f32 = functools.partial(jax.ShapeDtypeStruct, dtype=jnp.float32)
    return call(
        functools.partial(backward_kernel, total_rows),
        (f32((members, 2, rows // 2, LANES)), f32((rows // 2, LANES))),
        [
            pltpu.VMEM((rows + 2 * HALO, chans, width), jnp.bfloat16),
            pltpu.VMEM((rows + HALO, own, width), jnp.float32),
            pltpu.VMEM((rows + HALO, chans, width), jnp.bfloat16),
            pltpu.VMEM((LANES, LANES), jnp.float32),
            pltpu.VMEM((LANES, width + LANES), jnp.float32),
            pltpu.VMEM((slots * rows, LANES), jnp.float32),
        ],
        2 * 15 * chans * chans * width * 40,
        scalars, cot_behind, cot, cot_ahead, slope_0, slope_1, taps,
    )


def group_sizes(blocks, devices):
    members = blocks // 2
    return members, devices // members


def exchange_in_group(chunks):
    members = chunks.shape[0]
    count = lax.axis_size("chrom")
    lists = [[q * members + k for k in range(members)] for q in range(count // members)]
    return lax.all_to_all(chunks, "chrom", 0, 0, axis_index_groups=lists)


def exchange_across_groups(chunks, members):
    groups = chunks.shape[0] // 2
    lists = [
        [2 * (t * members + r) + c for t in range(groups) for c in range(2)] for r in range(members)
    ]
    return lax.all_to_all(chunks, ("chrom", "chan"), 0, 0, axis_index_groups=lists)


def window_terms(proj, members, groups, group, member, chan):
    own = proj.shape[1] // 2
    half = proj.shape[0] // 2
    tile = jnp.pad(jnp.concatenate((proj[:half], proj[half:]), axis=1), ((0, 0), (0, LANES - 4 * own)))
    held = exchange_across_groups(jnp.broadcast_to(tile, (2 * groups, half, LANES)), members)
    held = held.reshape(groups, 2, half, LANES)
    held = jnp.where(chan == 0, held, held[:, ::-1])
    held = lax.dynamic_slice_in_dim(jnp.pad(held, ((1, 3), (0, 0), (0, 0), (0, 0))), group, 5, 0)

    def joined(first):
        pieces = [
            held[:, c, :, 2 * own * h + first : 2 * own * h + first + own] for h in range(2) for c in range(2)
        ]
        return jnp.concatenate(pieces, axis=2)

    near, far = joined(0), joined(own)
    to = jnp.arange(members, dtype=jnp.int32)[:, None, None, None]
    before = (member == members - 1) & (to == 0)
    after = (member == 0) & (to == members - 1)
    start = jnp.where(before, 0, jnp.where(member < to - 1, 2, 1))
    far = jnp.where(start == 0, far[None, 0:3], jnp.where(start == 1, far[None, 1:4], far[None, 2:5]))
    near = jnp.where(before, near[None, 0:1], jnp.where(after, near[None, 2:3], near[None, 1:2]))
    near = [near[:, :, :, SPARE * j : SPARE * (j + 1)] for j in range(3)]
    return exchange_in_group(jnp.concatenate((far, jnp.concatenate(near, axis=1)), axis=3))


def summed_terms(far_terms, near_terms, own, members, groups, group):
    part = jnp.sum(exchange_in_group(far_terms), axis=0)
    lanes = jnp.arange(LANES, dtype=jnp.int32)
    first = jnp.where(lanes < 2 * own, part[0], near_terms)
    second = jnp.where(lanes < 2 * own, jnp.roll(part[0], -2 * own, axis=1), 0)
    to = jnp.arange(groups, dtype=jnp.int32)[:, None, None, None]
    chunks = jnp.where(
        to == group, first, jnp.where(to == group + 1, second, jnp.where(to == group + 2, part[1], 0))
    )
    chunks = jnp.broadcast_to(chunks, (groups, 2) + part.shape[1:])
    recv = exchange_across_groups(chunks.reshape((2 * groups,) + part.shape[1:]), members)
    return jnp.sum(recv.reshape(chunks.shape), axis=0)


def shards(
    embedding, window_start, band_width, dilations, near_weight, far_weight,
    distance_bias, conv_weight, conv_bias, cotangent,
):
    rows = embedding.shape[0]
    own, width = distance_bias.shape
    chans = conv_weight.shape[2]
    features_half = embedding.shape[1] // 2
    chan = lax.axis_index("chan")
    place = lax.axis_index("chrom")
    first_row = place * rows
    total_rows = lax.axis_size("chrom") * rows
    members, groups = group_sizes(width // rows, lax.axis_size("chrom"))
    group, member = place // members, place % members
    row_ids = first_row + jnp.arange(rows, dtype=jnp.int32)
    scalars = jnp.stack([band_width[0], first_row, dilations[0], dilations[1], member]).astype(jnp.int32)

    features = (
        embedding.astype(jnp.float32) + encode(row_ids, window_start[0], embedding.shape[1])
    ).astype(jnp.bfloat16)
    both = jnp.concatenate((near_weight, far_weight), axis=1)
    proj = jnp.dot(features, both, preferred_element_type=jnp.float32)
    terms = window_terms(proj, members, groups, group, member, chan)

    cot_other = from_partner(cotangent)
    offsets = jnp.arange(width, dtype=jnp.int32)
    keep = (offsets[None, :] < band_width[0]) & (row_ids[:, None] + offsets[None, :] < total_rows)
    cot = jnp.concatenate((cotangent, cot_other), axis=0)
    cot = jnp.where(keep[:, None, :], jnp.swapaxes(cot, 0, 1), 0).astype(jnp.bfloat16)
    cot, terms = lax.optimization_barrier((cot, terms))
    cot_behind = from_ahead(cot, -1)
    cot_ahead = from_ahead(cot, 1)

    small = jnp.concatenate((distance_bias, conv_bias.T, jnp.zeros((own, LANES - 2), jnp.float32)), axis=1)
    params = jnp.concatenate((small, from_partner(small)), axis=0)
    other = from_partner(lax.dynamic_slice_in_dim(both, (1 - chan) * features_half, features_half, 0))
    here = lax.dynamic_slice_in_dim(both, chan * features_half, features_half, 0)
    back_project = []
    for cols in (jnp.where(chan == 0, here, other), jnp.where(chan == 0, other, here)):
        near_rows, far_rows = cols[:, :own].T, cols[:, own:].T
        gap = jnp.zeros((own, features_half), cols.dtype)
        rest = jnp.zeros((LANES - 4 * own, 2 * features_half), cols.dtype)
        for block in (far_rows, near_rows):
            back_project.append(jnp.concatenate((block, gap), axis=1))
            back_project.append(jnp.concatenate((gap, block), axis=1))
        back_project.append(rest)
    back_project = jnp.concatenate(back_project, axis=0)

    twice = jnp.concatenate((conv_weight, conv_weight), axis=2)
    twice = jnp.concatenate((twice, twice), axis=3)
    turned = lax.dynamic_slice(twice, (0, 0, chan * own, chan * own), conv_weight.shape)
    last = jnp.zeros((-5 * own % 16, 3 * chans), conv_weight.dtype)
    taps_ahead = jnp.concatenate(
        (stacked_taps(turned[0], 1, chans), stacked_taps(turned[1], 1, own), last), axis=0
    )
    taps_back = jnp.concatenate(
        (stacked_taps(turned[1], -1, chans), stacked_taps(turned[0], -1, own), last), axis=0
    )

    pair_rows, slope_0, slope_1 = forward_call(total_rows, rows, scalars, terms, params, taps_ahead)
    pair_out = jnp.swapaxes(pair_rows.astype(jnp.bfloat16), 0, 1)
    far_terms, near_terms = backward_call(
        total_rows, members, scalars, cot_behind, cot, cot_ahead, slope_0, slope_1, taps_back
    )
    sums = summed_terms(far_terms, near_terms, own, members, groups, group)
    lows = jnp.concatenate((sums[0], sums[1]), axis=1).astype(jnp.bfloat16)
    grads = jnp.dot(lows, back_project, preferred_element_type=jnp.float32)
    grads = jnp.concatenate((grads[:, :features_half], grads[:, features_half:]), axis=0)
    return (pair_out, grads.astype(jnp.bfloat16))


def solution(mesh):
    in_specs = (
        P("chrom", None),
        P(),
        P(),
        P(),
        P(None, "chan"),
        P(None, "chan"),
        P("chan", None),
        P(),
        P(None, "chan"),
        P("chan", "chrom", None),
    )
    out_specs = (P("chan", "chrom", None), P("chrom", "chan"))
    return jax.shard_map(shards, mesh=mesh, in_specs=in_specs, out_specs=out_specs, check_vma=False)
```

```python
import functools

import jax
import jax.numpy as jnp
from jax import lax
from jax.experimental import pallas as pl
from jax.experimental.pallas import tpu as pltpu
from jax.sharding import PartitionSpec as P

DMAX = 8
NF = 16
HALO = 2 * DMAX
LANES = 128
SPARE = 32
SHIFTS = (-2, -1, 0, 1, 2)
GROUP = 8
SEEDS = 4

two_pi = 6.283185307179586
inv_sqrt2 = 0.7071067811865476
inv_sqrt_2pi = 0.3989422804014327


def encode(row_ids, start_bin, feature_count):
    octave = jnp.arange(NF, dtype=jnp.int32)
    period = jnp.power(jnp.int32(2), octave + 2).astype(jnp.int32)
    residue = jnp.remainder(start_bin + row_ids[:, None], period[None, :])
    angles = residue.astype(jnp.float32) * (two_pi / period.astype(jnp.float32))[None, :]
    encoding = jnp.concatenate((jnp.sin(angles), jnp.cos(angles)), axis=1)
    return jnp.pad(encoding, ((0, 0), (0, feature_count - 2 * NF)))


def from_ahead(block, distance):
    devices = range(lax.axis_size("chrom"))
    route = [(i + distance, i) for i in devices if i + distance in devices]
    return lax.ppermute(block, "chrom", route)


def after(block, earlier):
    return lax.optimization_barrier((block, earlier))[0]


def from_partner(block):
    return lax.ppermute(block, "chan", [(0, 1), (1, 0)])


def stacked_taps(kernel, sign, out_count):
    chan_count = kernel.shape[1]
    rows = []
    for m in SHIFTS:
        blocks = []
        for a in (-1, 0, 1):
            b = a + m
            if -1 <= b <= 1:
                tap = kernel[3 * (sign * a + 1) + sign * b + 1]
                blocks.append((tap if sign > 0 else tap.T)[:out_count])
            else:
                blocks.append(jnp.zeros((out_count, chan_count), kernel.dtype))
        rows.append(jnp.concatenate(blocks, axis=1))
    return jnp.concatenate(rows, axis=0)


def lane_ids():
    return lax.broadcasted_iota(jnp.int32, (1, LANES), 1)


def tiles_of(values):
    return [values[:, k : k + LANES] for k in range(0, values.shape[1], LANES)]


def pull(tiles, amount, count, lanes):
    turned = [pltpu.roll(tile, lax.rem(LANES - amount, LANES), 1) for tile in tiles]
    turned.append(jnp.zeros_like(turned[0]))
    inside = lanes < LANES - amount
    return [jnp.where(inside, turned[k], turned[k + 1]) for k in range(count)]


def push(tiles, amount, count, lanes):
    zero = jnp.zeros_like(tiles[0])
    turned = [zero] + [pltpu.roll(tile, amount, 1) for tile in tiles] + [zero]
    inside = lanes >= amount
    return [jnp.where(inside, turned[k + 1], turned[k]) for k in range(count)]


def tap_sums(weights, ref, first, dilation, out_count, lanes):
    width = ref.shape[2]
    count = width // LANES
    window = jnp.concatenate(
        [
            jnp.concatenate([ref[first + g + a * dilation] for a in (-1, 0, 1)], axis=0)
            for g in range(GROUP)
        ],
        axis=1,
    )
    stacked = jnp.dot(weights[...], window, preferred_element_type=jnp.float32)
    sums = []
    for g in range(GROUP):
        part = [
            tiles_of(stacked[k * out_count : (k + 1) * out_count, g * width : (g + 1) * width])
            for k in range(5)
        ]
        shifted = [
            push(part[0], 2 * dilation, count, lanes),
            push(part[1], dilation, count, lanes),
            part[2],
            pull(part[3], dilation, count, lanes),
            pull(part[4], 2 * dilation, count, lanes),
        ]
        sums.append([sum(tile[1:], tile[0]) for tile in zip(*shifted)])
    return sums


def limit_of(row, first_row, band_width, total_rows):
    here = first_row - HALO + row
    return jnp.where(here < 0, 0, jnp.minimum(band_width, total_rows - here))


def gelu_cdf(values):
    return 0.5 + 0.5 * lax.erf(values * inv_sqrt2)


def gelu_slope(values, cdf):
    return cdf + values * (inv_sqrt_2pi * jnp.exp(-0.5 * values * values))


def forward_kernel(
    total_rows, scalars, terms, bias_other, bias_here, conv_bias, taps,
    pair_out, slope_0, slope_1, pair_0, act_0, act_1, pair_1, far_rows, near_rows, far, near, bias,
):
    band_width, first_row, step_0, step_1, member = (scalars[k] for k in range(5))
    lanes = lane_ids()
    rows, own, width = pair_out.shape
    chans = 2 * own
    count = width // LANES
    members = terms.shape[0]
    taps_0, taps_1 = taps.at[: 5 * chans], taps.at[5 * chans :]
    slabs = own // 8
    per_tile = LANES // SPARE

    bias[:own] = bias_here[...]
    for k in range(count):
        for j in range(slabs):
            block = jnp.zeros((8, LANES), jnp.float32)
            for t in range(per_tile):
                piece = pltpu.roll(bias_other[k * per_tile + t], (t - j) % per_tile * SPARE, 1)
                block = jnp.where(lanes // SPARE == t, piece, block)
            bias[own + 8 * j : own + 8 * (j + 1), k * LANES : (k + 1) * LANES] = block
    first = slabs * SPARE
    bias_0 = jnp.concatenate(
        [conv_bias[:, 0:1]] + [bias_other[0, :, first + j : first + j + 1] for j in range(slabs)], axis=0
    )
    bias_1 = conv_bias[:, 1:2]

    far_rows[...] = jnp.zeros_like(far_rows)
    near_rows[...] = jnp.zeros_like(near_rows)
    half = rows // 2
    for place in range(width // rows + 3):
        source = lax.rem(member + (members - 1 + place), members)
        tile = terms[source, place // members]
        far_rows[place * rows : place * rows + half] = tile
        far_rows[place * rows + half : (place + 1) * rows] = pltpu.roll(tile, LANES - chans, 1)
        if place < 3:
            tile = jnp.zeros((half, LANES), jnp.float32)
            for j in range(3):
                part = pltpu.roll(terms[source, j], SPARE * (j + 1), 1)
                tile = jnp.where(lanes // SPARE == j, part, tile)
            near_rows[place * rows : place * rows + half] = tile
            near_rows[place * rows + half : (place + 1) * rows] = pltpu.roll(tile, LANES - chans, 1)
    for k in range(count + 1):
        span = slice(k * LANES, (k + 1) * LANES)
        far[:, span] = far_rows[span].T[:chans]
    near[...] = near_rows[...].T[:chans]

    def keeps(row):
        limit = limit_of(row, first_row, band_width, total_rows)
        return [lanes + k * LANES < limit for k in range(count)]

    def seed(row, with_slope):
        near_col = pltpu.roll(near[...], lax.rem(LANES - row, LANES), 1)[:, 0:1]
        ahead = pull(tiles_of(far[...]), row, count, lanes)
        for k, keep in enumerate(keeps(row)):
            span = pl.ds(k * LANES, LANES)
            value = jnp.where(keep, near_col + ahead[k] + bias[:, span], 0.0)
            cdf = gelu_cdf(value)
            pair_0[row, :, span] = value
            act_0[row, :, span] = (value * cdf).astype(jnp.bfloat16)
            if with_slope:
                slope_0[row - HALO, :, span] = gelu_slope(value[:own], cdf[:own])

    def outer_seeds(block, _):
        for g in range(SEEDS):
            index = block * SEEDS + g
            seed(jnp.where(index < HALO, index, index + rows), False)
        return 0

    def inner_seeds(block, _):
        for g in range(SEEDS):
            seed(block * SEEDS + g + HALO, True)
        return 0

    lax.fori_loop(0, 2 * HALO // SEEDS, outer_seeds, 0)
    lax.fori_loop(0, rows // SEEDS, inner_seeds, 0)

    def layer_0(block, _):
        first = block * GROUP
        convs = tap_sums(taps_0, act_0, first + DMAX, step_0, chans, lanes)
        for g, conv in enumerate(convs):
            index = first + g
            row = index + DMAX
            for k, keep in enumerate(keeps(row)):
                span = pl.ds(k * LANES, LANES)
                value = jnp.where(keep, pair_0[row, :, span] + conv[k] + bias_0, 0.0)
                cdf = gelu_cdf(value)
                pair_1[index, :, span] = value[:own]
                act_1[index, :, span] = (value * cdf).astype(jnp.bfloat16)
                slope_1[index, :, span] = gelu_slope(value, cdf)
        return 0

    lax.fori_loop(0, (rows + HALO) // GROUP, layer_0, 0)

    def layer_1(block, _):
        first = block * GROUP
        convs = tap_sums(taps_1, act_1, first + DMAX, step_1, own, lanes)
        for g, conv in enumerate(convs):
            index = first + g
            for k, keep in enumerate(keeps(index + HALO)):
                span = pl.ds(k * LANES, LANES)
                value = jnp.where(keep, pair_1[index + DMAX, :, span] + conv[k] + bias_1, 0.0)
                pair_out[index, :, span] = value
        return 0

    lax.fori_loop(0, rows // GROUP, layer_1, 0)


def backward_kernel(
    total_rows, scalars, cot_behind, cot_here, cot_ahead, slope_0, slope_1, taps,
    far_terms, grad_2, grad_1, low_1, near_sum, far_sum, far_rows,
):
    band_width, first_row, step_0, step_1, member = (scalars[k] for k in range(5))
    lanes = lane_ids()
    rows, chans, width = cot_here.shape
    own = chans // 2
    count = width // LANES
    members = far_terms.shape[0]
    taps_1, taps_0 = taps.at[: 5 * chans], taps.at[5 * chans :]

    def keeps(row):
        limit = limit_of(row, first_row, band_width, total_rows)
        return [lanes + k * LANES < limit for k in range(count)]

    def lay(index, _):
        grad_2[index] = cot_behind[index]
        grad_2[index + rows] = cot_here[index]
        grad_2[index + 2 * rows] = cot_ahead[index]
        return 0

    lax.fori_loop(0, rows, lay, 0)

    def layer_1(block, _):
        first = block * GROUP
        convs = tap_sums(taps_1, grad_2, first + DMAX, step_1, chans, lanes)
        for g, conv in enumerate(convs):
            index = first + g
            row = index + DMAX
            for k, keep in enumerate(keeps(row)):
                span = pl.ds(k * LANES, LANES)
                above = grad_2[row, :, span].astype(jnp.float32)
                value = jnp.where(keep, above + slope_1[index, :, span] * conv[k], 0.0)
                grad_1[index, :, span] = value[:own]
                low_1[index, :, span] = value.astype(jnp.bfloat16)
        return 0

    lax.fori_loop(0, (rows + HALO) // GROUP, layer_1, 0)

    near_sum[...] = jnp.zeros_like(near_sum)
    far_sum[...] = jnp.zeros_like(far_sum)

    def layer_0(block, _):
        first = block * GROUP
        convs = tap_sums(taps_0, low_1, first + DMAX, step_0, own, lanes)
        for g, conv in enumerate(convs):
            index = first + g
            values = []
            for k, keep in enumerate(keeps(index + HALO)):
                span = pl.ds(k * LANES, LANES)
                above = grad_1[index + DMAX, :, span]
                values.append(jnp.where(keep, above + slope_0[index, :, span] * conv[k], 0.0))
            total = jnp.sum(sum(values[1:], values[0]), axis=1, keepdims=True)
            near_sum[:own] += jnp.where(lanes == index, total, 0.0)
            for k, tile in enumerate(push(values, index, count + 1, lanes)):
                far_sum[:own, k * LANES : (k + 1) * LANES] += tile
        return 0

    lax.fori_loop(0, rows // GROUP, layer_0, 0)

    far_rows[...] = jnp.zeros_like(far_rows)
    for k in range(count + 1):
        start = pl.multiple_of(member * rows, 8) + k * LANES
        far_rows[pl.ds(start, LANES)] = far_sum[:, k * LANES : (k + 1) * LANES].T
    half = rows // 2
    near_rows = near_sum[...].T
    near_terms = pltpu.roll(near_rows[:half], 2 * own, 1) + pltpu.roll(near_rows[half:rows], 3 * own, 1)

    def halves(slot):
        return [far_rows[slot * rows + h * half : slot * rows + (h + 1) * half] for h in range(2)]

    for r in range(members):
        pieces = halves(r) + halves(members + r)
        far_terms[r, 0] = sum(
            [pltpu.roll(piece, k * own, 1) for k, piece in enumerate(pieces) if k], pieces[0]
        )
        pieces = halves(2 * members + r)
        own_place = jnp.where(member == r, near_terms, 0.0)
        far_terms[r, 1] = pieces[0] + pltpu.roll(pieces[1], own, 1) + own_place


def call(kernel, out_shapes, scratch, flops, smem, *arrays):
    bytes_accessed = sum(a.size * a.dtype.itemsize for a in arrays)
    bytes_accessed += sum(s.size * s.dtype.itemsize for s in out_shapes)
    vmem = pl.BlockSpec(memory_space=pltpu.VMEM)
    return pl.pallas_call(
        kernel,
        out_shape=out_shapes,
        in_specs=[pl.BlockSpec(memory_space=pltpu.SMEM)] + [vmem] * len(arrays),
        out_specs=[vmem] * len(out_shapes),
        scratch_shapes=scratch,
        compiler_params=pltpu.CompilerParams(vmem_limit_bytes=32 * 2**20),
        cost_estimate=pl.CostEstimate(
            flops=flops, bytes_accessed=bytes_accessed, transcendentals=0
        ),
    )(smem, *arrays)


def forward_call(total_rows, rows, scalars, terms, bias_other, bias_here, conv_bias, taps):
    own, width = bias_here.shape
    chans = 2 * own
    f32 = functools.partial(jax.ShapeDtypeStruct, dtype=jnp.float32)
    return call(
        functools.partial(forward_kernel, total_rows),
        (f32((rows, own, width)), f32((rows, own, width)), f32((rows + HALO, chans, width))),
        [
            pltpu.VMEM((rows + 2 * HALO, chans, width), jnp.float32),
            pltpu.VMEM((rows + 2 * HALO, chans, width), jnp.bfloat16),
            pltpu.VMEM((rows + HALO, chans, width), jnp.bfloat16),
            pltpu.VMEM((rows + HALO, own, width), jnp.float32),
            pltpu.VMEM((width + LANES, LANES), jnp.float32),
            pltpu.VMEM((LANES, LANES), jnp.float32),
            pltpu.VMEM((chans, width + LANES), jnp.float32),
            pltpu.VMEM((chans, LANES), jnp.float32),
            pltpu.VMEM((chans, width), jnp.float32),
        ],
        2 * 15 * chans * chans * width * 40,
        scalars, terms, bias_other, bias_here, conv_bias, taps,
    )


def backward_call(total_rows, members, scalars, cot_behind, cot, cot_ahead, slope_0, slope_1, taps):
    rows, chans, width = cot.shape
    own = chans // 2
    slots = members + (width + LANES) // rows
    f32 = functools.partial(jax.ShapeDtypeStruct, dtype=jnp.float32)
    return call(
        functools.partial(backward_kernel, total_rows),
        (f32((members, 2, rows // 2, LANES)),),
        [
            pltpu.VMEM((rows + 2 * HALO, chans, width), jnp.bfloat16),
            pltpu.VMEM((rows + HALO, own, width), jnp.float32),
            pltpu.VMEM((rows + HALO, chans, width), jnp.bfloat16),
            pltpu.VMEM((LANES, LANES), jnp.float32),
            pltpu.VMEM((LANES, width + LANES), jnp.float32),
            pltpu.VMEM((slots * rows, LANES), jnp.float32),
        ],
        2 * 15 * chans * chans * width * 40,
        scalars, cot_behind, cot, cot_ahead, slope_0, slope_1, taps,
    )


def group_sizes(blocks, devices):
    members = blocks // 2
    return members, devices // members


def exchange_in_group(chunks, both_halves=False):
    members = chunks.shape[0]
    count = lax.axis_size("chrom")
    if not both_halves:
        lists = [[q * members + k for k in range(members)] for q in range(count // members)]
        return lax.all_to_all(chunks, "chrom", 0, 0, axis_index_groups=lists)
    lists = [
        [2 * (q * members + k) + c for k in range(members) for c in range(2)]
        for q in range(count // members)
    ]
    twice = jnp.broadcast_to(chunks[:, None], (members, 2) + chunks.shape[1:])
    twice = twice.reshape((2 * members,) + chunks.shape[1:])
    recv = lax.all_to_all(twice, ("chrom", "chan"), 0, 0, axis_index_groups=lists)
    return recv.reshape((members, 2) + chunks.shape[1:])


def exchange_across_groups(chunks, members):
    groups = chunks.shape[0] // 2
    lists = [
        [2 * (t * members + r) + c for t in range(groups) for c in range(2)] for r in range(members)
    ]
    return lax.all_to_all(chunks, ("chrom", "chan"), 0, 0, axis_index_groups=lists)


def window_terms(proj, distance_bias, conv_bias, members, groups, group, member, chan):
    own = proj.shape[1] // 2
    half = proj.shape[0] // 2
    slabs = own // 8
    tile = jnp.concatenate((proj[:half], proj[half:]), axis=1)
    tile = jnp.pad(tile, ((0, 0), (0, LANES - tile.shape[1])))
    piece = lax.dynamic_slice_in_dim(distance_bias, group * SPARE, SPARE, 1)
    piece = [piece[8 * j : 8 * (j + 1)] for j in range(slabs)] + [conv_bias[0].reshape(slabs, 8).T]
    piece = jnp.concatenate(piece, axis=1)
    piece = jnp.pad(piece, ((0, 0), (0, LANES - piece.shape[1])))
    sent = jnp.broadcast_to(jnp.stack((tile, piece)), (2 * groups, 2, half, LANES))
    recv = exchange_across_groups(sent, members).reshape(groups, 2, 2, half, LANES)
    bias_other = lax.dynamic_index_in_dim(recv, 1 - chan, 1, keepdims=False)[:, 1]
    held = recv[:, :, 0]
    held = jnp.where(chan == 0, held, held[:, ::-1])
    held = lax.dynamic_slice_in_dim(jnp.pad(held, ((1, 3), (0, 0), (0, 0), (0, 0))), group, 5, 0)

    def joined(first):
        pieces = [
            held[:, c, :, 2 * own * h + first : 2 * own * h + first + own] for h in range(2) for c in range(2)
        ]
        return jnp.concatenate(pieces, axis=2)

    near, far = joined(0), joined(own)
    to = jnp.arange(members, dtype=jnp.int32)[:, None, None, None]
    before = (member == members - 1) & (to == 0)
    after = (member == 0) & (to == members - 1)
    start = jnp.where(before, 0, jnp.where(member < to - 1, 2, 1))
    far = jnp.where(start == 0, far[None, 0:3], jnp.where(start == 1, far[None, 1:4], far[None, 2:5]))
    near = jnp.where(before, near[None, 0:1], jnp.where(after, near[None, 2:3], near[None, 1:2]))
    near = [near[:, :, :, SPARE * j : SPARE * (j + 1)] for j in range(3)]
    return sent, jnp.concatenate((far, jnp.concatenate(near, axis=1)), axis=3), bias_other


def summed_terms(chunks, own):
    members = chunks.shape[0]
    part = jnp.sum(exchange_in_group(chunks, both_halves=True), axis=0)
    ahead_1 = from_ahead(part[:, 0], -members)
    ahead_2 = from_ahead(part[:, 1], -2 * members)
    lanes = jnp.arange(LANES, dtype=jnp.int32)
    far = part[:, 0] + jnp.roll(ahead_1, -2 * own, axis=2) + ahead_2
    return jnp.where(lanes < 2 * own, far, jnp.where(lanes < 4 * own, part[:, 1], 0))


def shards(
    embedding, window_start, band_width, dilations, near_weight, far_weight,
    distance_bias, conv_weight, conv_bias, cotangent,
):
    rows = embedding.shape[0]
    own, width = distance_bias.shape
    chans = conv_weight.shape[2]
    features_half = embedding.shape[1] // 2
    chan = lax.axis_index("chan")
    place = lax.axis_index("chrom")
    first_row = place * rows
    total_rows = lax.axis_size("chrom") * rows
    members, groups = group_sizes(width // rows, lax.axis_size("chrom"))
    group, member = place // members, place % members
    row_ids = first_row + jnp.arange(rows, dtype=jnp.int32)
    scalars = jnp.stack([band_width[0], first_row, dilations[0], dilations[1], member]).astype(jnp.int32)

    features = (
        embedding.astype(jnp.float32) + encode(row_ids, window_start[0], embedding.shape[1])
    ).astype(jnp.bfloat16)
    both = jnp.concatenate((near_weight, far_weight), axis=1)
    proj = jnp.dot(features, both, preferred_element_type=jnp.float32)
    sent, chunks, bias_other = window_terms(
        proj, distance_bias, conv_bias, members, groups, group, member, chan
    )
    terms = exchange_in_group(chunks)

    def weight_rows(half):
        parts = [
            lax.dynamic_slice_in_dim(w, half * features_half, features_half, 0).T
            for w in (near_weight, far_weight)
        ]
        return jnp.concatenate(parts, axis=1)

    cot_here = jnp.swapaxes(cotangent, 0, 1)
    mixed = jnp.concatenate((cot_here, weight_rows(1 - chan)[None]), axis=0)
    mixed = from_partner(after(mixed, sent))
    offsets = jnp.arange(width, dtype=jnp.int32)
    keep = (offsets[None, :] < band_width[0]) & (row_ids[:, None] + offsets[None, :] < total_rows)
    mixed = after(mixed, terms)
    cot = jnp.concatenate((cot_here, mixed[:rows]), axis=1)
    cot = jnp.where(keep[:, None, :], cot, 0).astype(jnp.bfloat16)
    cot_behind = from_ahead(cot, -1)
    cot_ahead = from_ahead(cot, 1)

    here, other = weight_rows(chan), mixed[rows]
    back_project = []
    for cols in (jnp.where(chan == 0, here, other), jnp.where(chan == 0, other, here)):
        near_rows, far_rows = cols[:, :features_half], cols[:, features_half:]
        gap = jnp.zeros((own, features_half), cols.dtype)
        rest = jnp.zeros((LANES - 4 * own, 2 * features_half), cols.dtype)
        for block in (far_rows, near_rows):
            back_project.append(jnp.concatenate((block, gap), axis=1))
            back_project.append(jnp.concatenate((gap, block), axis=1))
        back_project.append(rest)
    back_project = jnp.concatenate(back_project, axis=0)

    twice = jnp.concatenate((conv_weight, conv_weight), axis=2)
    twice = jnp.concatenate((twice, twice), axis=3)
    turned = lax.dynamic_slice(twice, (0, 0, chan * own, chan * own), conv_weight.shape)
    last = jnp.zeros((-5 * own % 16, 3 * chans), conv_weight.dtype)
    taps_ahead = jnp.concatenate(
        (stacked_taps(turned[0], 1, chans), stacked_taps(turned[1], 1, own), last), axis=0
    )
    taps_back = jnp.concatenate(
        (stacked_taps(turned[1], -1, chans), stacked_taps(turned[0], -1, own), last), axis=0
    )

    pair_rows, slope_0, slope_1 = forward_call(
        total_rows, rows, scalars, terms, bias_other, distance_bias, conv_bias.T, taps_ahead
    )
    pair_out = jnp.swapaxes(pair_rows.astype(jnp.bfloat16), 0, 1)
    (terms_back,) = backward_call(
        total_rows, members, scalars, cot_behind, cot, cot_ahead, slope_0, slope_1, taps_back
    )
    sums = summed_terms(terms_back, own)
    lows = jnp.concatenate((sums[0], sums[1]), axis=1).astype(jnp.bfloat16)
    grads = jnp.dot(lows, back_project, preferred_element_type=jnp.float32)
    grads = jnp.concatenate((grads[:, :features_half], grads[:, features_half:]), axis=0)
    return (pair_out, grads.astype(jnp.bfloat16))


def solution(mesh):
    in_specs = (
        P("chrom", None),
        P(),
        P(),
        P(),
        P(None, "chan"),
        P(None, "chan"),
        P("chan", None),
        P(),
        P(None, "chan"),
        P("chan", "chrom", None),
    )
    out_specs = (P("chan", "chrom", None), P("chrom", "chan"))
    return jax.shard_map(shards, mesh=mesh, in_specs=in_specs, out_specs=out_specs, check_vma=False)
```

```python
import functools

import jax
import jax.numpy as jnp
from jax import lax
from jax.experimental import pallas as pl
from jax.experimental.pallas import tpu as pltpu
from jax.sharding import PartitionSpec as P

DMAX = 8
NF = 16
HALO = 2 * DMAX
LANES = 128
SPARE = 32
SHIFTS = (-2, -1, 0, 1, 2)
GROUP = 8
SEEDS = 4

two_pi = 6.283185307179586
inv_sqrt2 = 0.7071067811865476
inv_sqrt_2pi = 0.3989422804014327


def encode(row_ids, start_bin, feature_count):
    octave = jnp.arange(NF, dtype=jnp.int32)
    period = jnp.power(jnp.int32(2), octave + 2).astype(jnp.int32)
    residue = jnp.remainder(start_bin + row_ids[:, None], period[None, :])
    angles = residue.astype(jnp.float32) * (two_pi / period.astype(jnp.float32))[None, :]
    encoding = jnp.concatenate((jnp.sin(angles), jnp.cos(angles)), axis=1)
    return jnp.pad(encoding, ((0, 0), (0, feature_count - 2 * NF)))


def from_ahead(block, distance):
    devices = range(lax.axis_size("chrom"))
    route = [(i + distance, i) for i in devices if i + distance in devices]
    return lax.ppermute(block, "chrom", route)


def after(block, earlier):
    return lax.optimization_barrier((block, earlier))[0]


def from_partner(block):
    return lax.ppermute(block, "chan", [(0, 1), (1, 0)])


def stacked_taps(kernel, sign, out_count):
    chan_count = kernel.shape[1]
    rows = []
    for m in SHIFTS:
        blocks = []
        for a in (-1, 0, 1):
            b = a + m
            if -1 <= b <= 1:
                tap = kernel[3 * (sign * a + 1) + sign * b + 1]
                blocks.append((tap if sign > 0 else tap.T)[:out_count])
            else:
                blocks.append(jnp.zeros((out_count, chan_count), kernel.dtype))
        rows.append(jnp.concatenate(blocks, axis=1))
    return jnp.concatenate(rows, axis=0)


def lane_ids():
    return lax.broadcasted_iota(jnp.int32, (1, LANES), 1)


def tiles_of(values):
    return [values[:, k : k + LANES] for k in range(0, values.shape[1], LANES)]


def pull(tiles, amount, count, lanes):
    turned = [pltpu.roll(tile, lax.rem(LANES - amount, LANES), 1) for tile in tiles]
    turned.append(jnp.zeros_like(turned[0]))
    inside = lanes < LANES - amount
    return [jnp.where(inside, turned[k], turned[k + 1]) for k in range(count)]


def push(tiles, amount, count, lanes):
    zero = jnp.zeros_like(tiles[0])
    turned = [zero] + [pltpu.roll(tile, amount, 1) for tile in tiles] + [zero]
    inside = lanes >= amount
    return [jnp.where(inside, turned[k + 1], turned[k]) for k in range(count)]


def tap_sums(weights, ref, first, dilation, out_count, lanes):
    width = ref.shape[2]
    count = width // LANES
    window = jnp.concatenate(
        [
            jnp.concatenate([ref[first + g + a * dilation] for a in (-1, 0, 1)], axis=0)
            for g in range(GROUP)
        ],
        axis=1,
    )
    stacked = jnp.dot(weights[...], window, preferred_element_type=jnp.float32)
    sums = []
    for g in range(GROUP):
        part = [
            tiles_of(stacked[k * out_count : (k + 1) * out_count, g * width : (g + 1) * width])
            for k in range(5)
        ]
        shifted = [
            push(part[0], 2 * dilation, count, lanes),
            push(part[1], dilation, count, lanes),
            part[2],
            pull(part[3], dilation, count, lanes),
            pull(part[4], 2 * dilation, count, lanes),
        ]
        sums.append([sum(tile[1:], tile[0]) for tile in zip(*shifted)])
    return sums


def limit_of(row, first_row, band_width, total_rows):
    here = first_row - HALO + row
    return jnp.where(here < 0, 0, jnp.minimum(band_width, total_rows - here))


def gelu_cdf(values):
    return 0.5 + 0.5 * lax.erf(values * inv_sqrt2)


def gelu_slope(values, cdf):
    return cdf + values * (inv_sqrt_2pi * jnp.exp(-0.5 * values * values))


def fetch(sems, *pairs):
    copies = [pltpu.make_async_copy(a, b, sems.at[k]) for k, (a, b) in enumerate(pairs)]
    for copy in copies:
        copy.start()
    for copy in copies:
        copy.wait()


def lay_slabs(target, row, slabs):
    lanes = lane_ids()
    per_tile = LANES // SPARE
    for j, pieces in enumerate(slabs):
        for k in range(0, len(pieces), per_tile):
            block = jnp.zeros((8, LANES), jnp.float32)
            for t, (tile, at) in enumerate(pieces[k : k + per_tile]):
                block = jnp.where(lanes // SPARE == t, pltpu.roll(tile, (t - at) % per_tile * SPARE, 1), block)
            target[row + 8 * j : row + 8 * (j + 1), k * SPARE : k * SPARE + LANES] = block


def chunk_kernel(scalars, tile, ahead_1, ahead_2, edge, conv_bias, bias, weights, chunks, last_slab):
    member = scalars[4]
    lanes = lane_ids()
    members = chunks.shape[0]
    own = bias.shape[0]
    wide = 2 * own
    slabs = own // 8

    def slabs_of(ref):
        turn = lax.rem(ref.shape[1] - member * SPARE, ref.shape[1])
        piece = pltpu.roll(ref[...], turn, 1)[:, :LANES]
        return [piece[8 * j : 8 * (j + 1)] for j in range(slabs)]

    weight = [pltpu.roll(slab, 3 * SPARE, 1) for slab in slabs_of(weights)]
    last_slab[...] = jnp.where(lanes >= 3 * SPARE, weight[2], 0.0)
    third = jnp.zeros((8, LANES), jnp.float32)
    for j, slab in enumerate(slabs_of(bias)):
        third = jnp.where(lanes // SPARE == j, pltpu.roll(slab, j * SPARE, 1), third)
        third = jnp.where(lanes == slabs * SPARE + j, conv_bias[8 * j : 8 * (j + 1), 0:1], third)
    held = [edge[...], tile[...], ahead_1[...], ahead_2[...], edge[...]]
    first = [pltpu.roll(block, LANES - wide, 1) for block in held]
    near = [pltpu.roll(block, wide, 1) for block in held[:3]]
    one = [jnp.where(lanes < wide, first[k], jnp.where(lanes < 2 * wide, held[k + 1], weight[0])) for k in range(3)]
    for to in range(members):
        before = (member == members - 1) & (to == 0)
        after_last = (member == 0) & (to == members - 1)
        start = jnp.where(before, 0, jnp.where(member < to - 1, 2, 1))

        def chosen(blocks):
            return jnp.where(start == 0, blocks[0], jnp.where(start == 1, blocks[1], blocks[2]))

        near_to = jnp.where(before, near[0], jnp.where(after_last, near[2], near[1]))
        two = jnp.where(lanes < wide, chosen(first[2:]), jnp.where(lanes < 2 * wide, near_to, weight[1]))
        one_to = chosen(one)
        for c in range(2):
            chunks[to, c, 0] = one_to
            chunks[to, c, 1] = two
            chunks[to, c, 2] = third


def last_kernel(scalars, part, ahead_1, ahead_2, terms, recv, weights, out, wide_weights, other):
    chan = scalars[5]
    lanes = lane_ids()
    own = weights.shape[0]
    wide = 2 * own
    half = weights.shape[1] // 2
    members = terms.shape[0]
    slabs = [[(terms[k, 1 - chan, j], 3) for k in range(members)] for j in range(2)]
    slabs.append([(recv[k, 1 - chan, 0], 3) for k in range(members)])
    lay_slabs(other, 0, slabs)
    total = jnp.zeros((part.shape[2], 2 * half), jnp.float32)
    wide_weights[...] = jnp.zeros_like(wide_weights)
    for source, c in ((weights, chan), (other, 1 - chan)):
        for k, block in enumerate((source[:, half:], source[:, :half])):
            wide_weights[2 * k * own : (2 * k + 1) * own, :half] = block
            wide_weights[(2 * k + 1) * own : (2 * k + 2) * own, half:] = block
        far = part[c, 0] + pltpu.roll(ahead_1[c], LANES - wide, 1) + ahead_2[c]
        sums = jnp.where(lanes < wide, far, jnp.where(lanes < 2 * wide, part[c, 1], 0.0))
        total += jnp.dot(
            sums.astype(jnp.bfloat16),
            wide_weights[...].astype(jnp.bfloat16),
            preferred_element_type=jnp.float32,
        )
    out[...] = jnp.concatenate((total[:, :half], total[:, half:]), axis=0).astype(out.dtype)


def forward_kernel(
    total_rows, scalars, conv_bias, terms_at, bias_at, taps_at,
    pair_out, slope_0, slope_1, pair_0, act_0, act_1, pair_1, far_rows, near_rows, far, near, bias,
    terms, taps, sems,
):
    band_width, first_row, step_0, step_1, member, chan = (scalars[k] for k in range(6))
    lanes = lane_ids()
    rows, own, width = pair_out.shape
    chans = 2 * own
    count = width // LANES
    members = terms.shape[0]
    taps_0, taps_1 = taps.at[: 5 * chans], taps.at[5 * chans :]
    fetch(sems, (terms_at, terms), (bias_at, bias.at[:own]), (taps_at, taps))
    slabs = own // 8

    lay_slabs(bias, own, [[(terms[k, 1 - chan, 2], j) for k in range(members)] for j in range(slabs)])
    last = terms[0, 1 - chan, 2]
    bias_0 = jnp.concatenate(
        [conv_bias[:, 0:1]] + [last[:, k : k + 1] for k in range(slabs * SPARE, slabs * SPARE + slabs)], axis=0
    )
    bias_1 = conv_bias[:, 1:2]

    far_rows[...] = jnp.zeros_like(far_rows)
    near_rows[...] = jnp.zeros_like(near_rows)
    half = rows // 2

    def lay_rows(target, place, source, tile, first):
        here, other = terms[source, chan, tile], terms[source, 1 - chan, tile]
        for h in range(2):
            from_lane = first + h * own
            joined = jnp.where(
                lanes < own,
                pltpu.roll(here, (LANES - from_lane) % LANES, 1),
                pltpu.roll(other, (LANES + own - from_lane) % LANES, 1),
            )
            target[place * rows + h * half : place * rows + (h + 1) * half] = joined

    for place in range(width // rows + 3):
        source = lax.rem(member + (members - 1 + place), members)
        j = place // members
        lay_rows(far_rows, place, source, j // 2, j % 2 * 2 * own)
        if place < 3:
            lay_rows(near_rows, place, source, 1, 2 * own)
    for k in range(count + 1):
        span = slice(k * LANES, (k + 1) * LANES)
        far[:, span] = far_rows[span].T[:chans]
    near[...] = near_rows[...].T[:chans]

    def keeps(row):
        limit = limit_of(row, first_row, band_width, total_rows)
        return [lanes + k * LANES < limit for k in range(count)]

    def seed(row, with_slope):
        near_col = pltpu.roll(near[...], lax.rem(LANES - row, LANES), 1)[:, 0:1]
        ahead = pull(tiles_of(far[...]), row, count, lanes)
        for k, keep in enumerate(keeps(row)):
            span = pl.ds(k * LANES, LANES)
            value = jnp.where(keep, near_col + ahead[k] + bias[:, span], 0.0)
            cdf = gelu_cdf(value)
            pair_0[row, :, span] = value
            act_0[row, :, span] = (value * cdf).astype(jnp.bfloat16)
            if with_slope:
                slope_0[row - HALO, :, span] = gelu_slope(value[:own], cdf[:own])

    def outer_seeds(block, _):
        for g in range(SEEDS):
            index = block * SEEDS + g
            seed(jnp.where(index < HALO, index, index + rows), False)
        return 0

    def inner_seeds(block, _):
        for g in range(SEEDS):
            seed(block * SEEDS + g + HALO, True)
        return 0

    lax.fori_loop(0, 2 * HALO // SEEDS, outer_seeds, 0)
    lax.fori_loop(0, rows // SEEDS, inner_seeds, 0)

    def layer_0(block, _):
        first = block * GROUP
        convs = tap_sums(taps_0, act_0, first + DMAX, step_0, chans, lanes)
        for g, conv in enumerate(convs):
            index = first + g
            row = index + DMAX
            for k, keep in enumerate(keeps(row)):
                span = pl.ds(k * LANES, LANES)
                value = jnp.where(keep, pair_0[row, :, span] + conv[k] + bias_0, 0.0)
                cdf = gelu_cdf(value)
                pair_1[index, :, span] = value[:own]
                act_1[index, :, span] = (value * cdf).astype(jnp.bfloat16)
                slope_1[index, :, span] = gelu_slope(value, cdf)
        return 0

    lax.fori_loop(0, (rows + HALO) // GROUP, layer_0, 0)

    def layer_1(block, _):
        first = block * GROUP
        convs = tap_sums(taps_1, act_1, first + DMAX, step_1, own, lanes)
        for g, conv in enumerate(convs):
            index = first + g
            for k, keep in enumerate(keeps(index + HALO)):
                span = pl.ds(k * LANES, LANES)
                value = jnp.where(keep, pair_1[index + DMAX, :, span] + conv[k] + bias_1, 0.0)
                pair_out[index, :, span] = value
        return 0

    lax.fori_loop(0, rows // GROUP, layer_1, 0)


def backward_kernel(
    total_rows, scalars, slope_0, slope_1, last_slab, cot_behind, cot_here, cot_ahead, taps_at,
    far_terms, grad_2, grad_1, low_1, near_sum, far_sum, far_rows, taps, sems,
):
    band_width, first_row, step_0, step_1, member = (scalars[k] for k in range(5))
    lanes = lane_ids()
    rows, chans, width = cot_here.shape
    own = chans // 2
    count = width // LANES
    members = far_terms.shape[0]
    taps_1, taps_0 = taps.at[: 5 * chans], taps.at[5 * chans :]

    def keeps(row):
        limit = limit_of(row, first_row, band_width, total_rows)
        return [lanes + k * LANES < limit for k in range(count)]

    fetch(
        sems,
        (cot_behind, grad_2.at[:rows]),
        (cot_here, grad_2.at[rows : 2 * rows]),
        (cot_ahead, grad_2.at[2 * rows :]),
        (taps_at, taps),
    )

    def layer_1(block, _):
        first = block * GROUP
        convs = tap_sums(taps_1, grad_2, first + DMAX, step_1, chans, lanes)
        for g, conv in enumerate(convs):
            index = first + g
            row = index + DMAX
            for k, keep in enumerate(keeps(row)):
                span = pl.ds(k * LANES, LANES)
                above = grad_2[row, :, span].astype(jnp.float32)
                value = jnp.where(keep, above + slope_1[index, :, span] * conv[k], 0.0)
                grad_1[index, :, span] = value[:own]
                low_1[index, :, span] = value.astype(jnp.bfloat16)
        return 0

    lax.fori_loop(0, (rows + HALO) // GROUP, layer_1, 0)

    near_sum[...] = jnp.zeros_like(near_sum)
    far_sum[...] = jnp.zeros_like(far_sum)

    def layer_0(block, _):
        first = block * GROUP
        convs = tap_sums(taps_0, low_1, first + DMAX, step_0, own, lanes)
        for g, conv in enumerate(convs):
            index = first + g
            values = []
            for k, keep in enumerate(keeps(index + HALO)):
                span = pl.ds(k * LANES, LANES)
                above = grad_1[index + DMAX, :, span]
                values.append(jnp.where(keep, above + slope_0[index, :, span] * conv[k], 0.0))
            total = jnp.sum(sum(values[1:], values[0]), axis=1, keepdims=True)
            near_sum[:own] += jnp.where(lanes == index, total, 0.0)
            for k, tile in enumerate(push(values, index, count + 1, lanes)):
                far_sum[:own, k * LANES : (k + 1) * LANES] += tile
        return 0

    lax.fori_loop(0, rows // GROUP, layer_0, 0)

    far_rows[...] = jnp.zeros_like(far_rows)
    for k in range(count + 1):
        start = pl.multiple_of(member * rows, 8) + k * LANES
        far_rows[pl.ds(start, LANES)] = far_sum[:, k * LANES : (k + 1) * LANES].T
    half = rows // 2
    near_rows = near_sum[...].T
    near_terms = pltpu.roll(near_rows[:half], 2 * own, 1) + pltpu.roll(near_rows[half:rows], 3 * own, 1)

    def halves(slot):
        return [far_rows[slot * rows + h * half : slot * rows + (h + 1) * half] for h in range(2)]

    for r in range(members):
        pieces = halves(r) + halves(members + r)
        one = sum([pltpu.roll(piece, k * own, 1) for k, piece in enumerate(pieces) if k], pieces[0])
        one = one + last_slab[...]
        pieces = halves(2 * members + r)
        own_place = jnp.where(member == r, near_terms, 0.0)
        two = pieces[0] + pltpu.roll(pieces[1], own, 1) + own_place
        for c in range(2):
            far_terms[r, c, 0] = one
            far_terms[r, c, 1] = two


def call(kernel, out_shapes, scratch, flops, smem, near_arrays, far_arrays=()):
    arrays = tuple(near_arrays) + tuple(far_arrays)
    bytes_accessed = sum(a.size * a.dtype.itemsize for a in arrays)
    bytes_accessed += sum(s.size * s.dtype.itemsize for s in out_shapes)
    vmem = pl.BlockSpec(memory_space=pltpu.VMEM)
    return pl.pallas_call(
        kernel,
        out_shape=out_shapes,
        in_specs=[pl.BlockSpec(memory_space=pltpu.SMEM)]
        + [vmem] * len(near_arrays)
        + [pl.BlockSpec(memory_space=pl.ANY)] * len(far_arrays),
        out_specs=[vmem] * len(out_shapes),
        scratch_shapes=scratch,
        compiler_params=pltpu.CompilerParams(vmem_limit_bytes=32 * 2**20),
        cost_estimate=pl.CostEstimate(
            flops=flops, bytes_accessed=bytes_accessed, transcendentals=0
        ),
    )(smem, *arrays)


f32 = functools.partial(jax.ShapeDtypeStruct, dtype=jnp.float32)


def chunk_call(members, scalars, tile, ahead_1, ahead_2, edge, conv_bias, bias, weights):
    return call(
        chunk_kernel,
        (f32((members, 2, 3) + tile.shape), f32(tile.shape)),
        [],
        0,
        scalars,
        (tile, ahead_1, ahead_2, edge, conv_bias, bias, weights),
    )


def last_call(scalars, part, ahead_1, ahead_2, terms, recv, weights):
    own, width = weights.shape
    (out,) = call(
        last_kernel,
        (jax.ShapeDtypeStruct((2 * part.shape[2], width // 2), jnp.bfloat16),),
        [pltpu.VMEM((LANES, width), jnp.float32), pltpu.VMEM((own, width), jnp.float32)],
        0,
        scalars,
        (part, ahead_1, ahead_2, terms, recv, weights),
    )
    return out


def forward_call(total_rows, rows, scalars, terms, bias_here, conv_bias, taps):
    own, width = bias_here.shape
    chans = 2 * own
    return call(
        functools.partial(forward_kernel, total_rows),
        (f32((rows, own, width)), f32((rows, own, width)), f32((rows + HALO, chans, width))),
        [
            pltpu.VMEM((rows + 2 * HALO, chans, width), jnp.float32),
            pltpu.VMEM((rows + 2 * HALO, chans, width), jnp.bfloat16),
            pltpu.VMEM((rows + HALO, chans, width), jnp.bfloat16),
            pltpu.VMEM((rows + HALO, own, width), jnp.float32),
            pltpu.VMEM((width + LANES, LANES), jnp.float32),
            pltpu.VMEM((LANES, LANES), jnp.float32),
            pltpu.VMEM((chans, width + LANES), jnp.float32),
            pltpu.VMEM((chans, LANES), jnp.float32),
            pltpu.VMEM((chans, width), jnp.float32),
            pltpu.VMEM(terms.shape, terms.dtype),
            pltpu.VMEM(taps.shape, taps.dtype),
            pltpu.SemaphoreType.DMA((3,)),
        ],
        2 * 15 * chans * chans * width * 40,
        scalars,
        (conv_bias,),
        (terms, bias_here, taps),
    )


def backward_call(total_rows, members, scalars, cot_behind, cot, cot_ahead, slope_0, slope_1, last_slab, taps):
    rows, chans, width = cot.shape
    own = chans // 2
    slots = members + (width + LANES) // rows
    (terms,) = call(
        functools.partial(backward_kernel, total_rows),
        (f32((members, 2, 2, rows // 2, LANES)),),
        [
            pltpu.VMEM((rows + 2 * HALO, chans, width), jnp.bfloat16),
            pltpu.VMEM((rows + HALO, own, width), jnp.float32),
            pltpu.VMEM((rows + HALO, chans, width), jnp.bfloat16),
            pltpu.VMEM((LANES, LANES), jnp.float32),
            pltpu.VMEM((LANES, width + LANES), jnp.float32),
            pltpu.VMEM((slots * rows, LANES), jnp.float32),
            pltpu.VMEM(taps.shape, taps.dtype),
            pltpu.SemaphoreType.DMA((4,)),
        ],
        2 * 15 * chans * chans * width * 40,
        scalars,
        (slope_0, slope_1, last_slab),
        (cot_behind, cot, cot_ahead, taps),
    )
    return terms


def exchange_in_group(chunks):
    members = chunks.shape[0]
    lists = [
        [2 * (q * members + k) + c for k in range(members) for c in range(2)]
        for q in range(lax.axis_size("chrom") // members)
    ]
    flat = chunks.reshape((2 * members,) + chunks.shape[2:])
    recv = lax.all_to_all(flat, ("chrom", "chan"), 0, 0, axis_index_groups=lists)
    return recv.reshape(chunks.shape)


def from_edges(block, members):
    count = lax.axis_size("chrom")
    route = [(i + 3 * members, i) for i in range(0, count - 3 * members, members)]
    route += [(i - members, i) for i in range(2 * members - 1, count, members)]
    return lax.ppermute(block, "chrom", route)


def projection_tile(features, near_weight, far_weight):
    half = features.shape[0] // 2
    parts = [jnp.dot(features, w, preferred_element_type=jnp.float32) for w in (near_weight, far_weight)]
    tile = jnp.concatenate([p[h * half : (h + 1) * half] for p in parts for h in range(2)], axis=1)
    return jnp.pad(tile, ((0, 0), (0, LANES - tile.shape[1])))


def shards(
    embedding, window_start, band_width, dilations, near_weight, far_weight,
    distance_bias, conv_weight, conv_bias, cotangent,
):
    rows = embedding.shape[0]
    own, width = distance_bias.shape
    chans = conv_weight.shape[2]
    features_half = embedding.shape[1] // 2
    chan = lax.axis_index("chan")
    place = lax.axis_index("chrom")
    first_row = place * rows
    total_rows = lax.axis_size("chrom") * rows
    members = width // rows // 2
    member = place % members
    row_ids = first_row + jnp.arange(rows, dtype=jnp.int32)
    scalars = jnp.stack([band_width[0], first_row, dilations[0], dilations[1], member, chan]).astype(jnp.int32)

    features = (
        embedding.astype(jnp.float32) + encode(row_ids, window_start[0], embedding.shape[1])
    ).astype(jnp.bfloat16)
    tile = projection_tile(features, near_weight, far_weight)
    ahead = from_ahead(tile, members), from_ahead(tile, 2 * members), from_edges(tile, members)

    def weight_rows(half):
        parts = [
            lax.dynamic_slice_in_dim(w, half * features_half, features_half, 0).T
            for w in (near_weight, far_weight)
        ]
        return jnp.concatenate(parts, axis=1).astype(jnp.float32)

    conv_columns = conv_bias.T
    chunks, last_slab = chunk_call(
        members, scalars, tile, *ahead, conv_columns, distance_bias, weight_rows(1 - chan)
    )
    terms = exchange_in_group(chunks)

    cot_other = from_partner(cotangent)
    offsets = jnp.arange(width, dtype=jnp.int32)
    keep = (offsets[None, :] < band_width[0]) & (row_ids[:, None] + offsets[None, :] < total_rows)
    cot = jnp.concatenate((cotangent, after(cot_other, chunks)), axis=0)
    cot = jnp.where(keep[:, None, :], jnp.swapaxes(cot, 0, 1), 0).astype(jnp.bfloat16)
    cot_behind = from_ahead(cot, -1)
    cot_ahead = from_ahead(cot, 1)

    conv_weight = after(conv_weight, chunks)
    twice = jnp.concatenate((conv_weight, conv_weight), axis=2)
    twice = jnp.concatenate((twice, twice), axis=3)
    turned = lax.dynamic_slice(twice, (0, 0, chan * own, chan * own), conv_weight.shape)
    last = jnp.zeros((-5 * own % 16, 3 * chans), conv_weight.dtype)
    taps_ahead = jnp.concatenate(
        (stacked_taps(turned[0], 1, chans), stacked_taps(turned[1], 1, own), last), axis=0
    )
    taps_back = jnp.concatenate(
        (stacked_taps(turned[1], -1, chans), stacked_taps(turned[0], -1, own), last), axis=0
    )

    pair_rows, slope_0, slope_1 = forward_call(
        total_rows, rows, scalars, terms, distance_bias, conv_columns, taps_ahead
    )
    pair_out = jnp.swapaxes(pair_rows.astype(jnp.bfloat16), 0, 1)
    terms_back = backward_call(
        total_rows, members, scalars, cot_behind, cot, cot_ahead, slope_0, slope_1, last_slab, taps_back
    )
    recv = exchange_in_group(terms_back)
    part = jnp.sum(recv, axis=0)
    ahead_1 = from_ahead(part[:, 0], -members)
    ahead_2 = from_ahead(part[:, 1], -2 * members)
    grads = last_call(scalars, part, ahead_1, ahead_2, terms, recv, weight_rows(chan))
    return (pair_out, grads)


def solution(mesh):
    in_specs = (
        P("chrom", None),
        P(),
        P(),
        P(),
        P(None, "chan"),
        P(None, "chan"),
        P("chan", None),
        P(),
        P(None, "chan"),
        P("chan", "chrom", None),
    )
    out_specs = (P("chan", "chrom", None), P("chrom", "chan"))
    return jax.shard_map(shards, mesh=mesh, in_specs=in_specs, out_specs=out_specs, check_vma=False)
```

```python
import functools

import jax
import jax.numpy as jnp
from jax import lax
from jax.experimental import pallas as pl
from jax.experimental.pallas import tpu as pltpu
from jax.sharding import PartitionSpec as P

DMAX = 8
NF = 16
HALO = 2 * DMAX
LANES = 128
SPARE = 32
GROUP = 16
GRANT = 60
SEEDS = 8

two_pi = 6.283185307179586
inv_sqrt2 = 0.7071067811865476
inv_sqrt_2pi = 0.3989422804014327


def from_ahead(block, distance):
    devices = range(lax.axis_size("chrom"))
    route = [(i + distance, i) for i in devices if i + distance in devices]
    return lax.ppermute(block, "chrom", route)


def after(block, earlier):
    return lax.optimization_barrier((block, earlier))[0]


def from_partner(block):
    return lax.ppermute(block, "chan", [(0, 1), (1, 0)])


def lane_ids():
    return lax.broadcasted_iota(jnp.int32, (1, LANES), 1)


def tiles_of(values):
    return [values[:, k : k + LANES] for k in range(0, values.shape[1], LANES)]


def pull(tiles, amount, count, lanes):
    turned = [pltpu.roll(tile, lax.rem(LANES - amount, LANES), 1) for tile in tiles]
    turned.append(jnp.zeros_like(turned[0]))
    inside = lanes < LANES - amount
    return [jnp.where(inside, turned[k], turned[k + 1]) for k in range(count)]


def push(tiles, amount, count, lanes):
    zero = jnp.zeros_like(tiles[0])
    turned = [zero] + [pltpu.roll(tile, amount, 1) for tile in tiles] + [zero]
    inside = lanes >= amount
    return [jnp.where(inside, turned[k + 1], turned[k]) for k in range(count)]


def tap_sums(weights, ref, first, dilation, out_count, lanes):
    width = ref.shape[2]
    count = width // LANES
    window = jnp.concatenate(
        [
            jnp.concatenate([ref[first + g + a * dilation] for a in (-1, 0, 1)], axis=0)
            for g in range(GROUP)
        ],
        axis=1,
    )
    stacked = jnp.dot(weights[...], window, preferred_element_type=jnp.float32)
    sums = []
    for g in range(GROUP):
        part = [
            tiles_of(stacked[k * out_count : (k + 1) * out_count, g * width : (g + 1) * width])
            for k in range(5)
        ]
        shifted = [
            push(part[0], 2 * dilation, count, lanes),
            push(part[1], dilation, count, lanes),
            part[2],
            pull(part[3], dilation, count, lanes),
            pull(part[4], 2 * dilation, count, lanes),
        ]
        sums.append([sum(tile[1:], tile[0]) for tile in zip(*shifted)])
    return sums


def limit_of(row, first_row, band_width, total_rows):
    here = first_row - HALO + row
    return jnp.where(here < 0, 0, jnp.minimum(band_width, total_rows - here))


def gelu_cdf(values):
    return 0.5 + 0.5 * lax.erf(values * inv_sqrt2)


def gelu_slope(values, cdf):
    return cdf + values * (inv_sqrt_2pi * jnp.exp(-0.5 * values * values))


def position(rows, members):
    place = lax.axis_index("chrom")
    return place * rows, lax.rem(place, members), lax.axis_index("chan")


def column(row):
    count = row.shape[1]
    same = [lax.broadcasted_iota(jnp.int32, (count, count), k) for k in range(2)]
    return jnp.sum(jnp.where(same[0] == same[1], row, 0.0), axis=1, keepdims=True)


def fetch(sems, *pairs):
    copies = [pltpu.make_async_copy(a, b, sems.at[k]) for k, (a, b) in enumerate(pairs)]
    for copy in copies:
        copy.start()
    for copy in copies:
        copy.wait()


def lay_slabs(target, row, slabs):
    lanes = lane_ids()
    per_tile = LANES // SPARE
    for j, pieces in enumerate(slabs):
        for k in range(0, len(pieces), per_tile):
            block = jnp.zeros((8, LANES), jnp.float32)
            for t, (tile, at) in enumerate(pieces[k : k + per_tile]):
                block = jnp.where(lanes // SPARE == t, pltpu.roll(tile, (t - at) % per_tile * SPARE, 1), block)
            target[row + 8 * j : row + 8 * (j + 1), k * SPARE : k * SPARE + LANES] = block


def tile_kernel(start, embedding_at, near_at, far_at, tile, embedding, near, far, weights, sems):
    fetch(sems, (embedding_at, embedding), (near_at, near), (far_at, far))
    rows = embedding.shape[0]
    own = near.shape[0]
    weights[...] = jnp.zeros_like(weights)
    for k, part in enumerate((near, near, far, far)):
        weights[k * own : (k + 1) * own] = part[...].astype(jnp.float32)
    lanes = lane_ids()
    first_row = lax.axis_index("chrom") * rows
    row_ids = start[0] + first_row + lax.broadcasted_iota(jnp.int32, (rows, LANES), 0)
    octave = lax.broadcasted_iota(jnp.int32, (rows, LANES), 1) % NF
    period = lax.shift_left(jnp.ones_like(octave), octave + 2)
    residue = row_ids & (period - 1)
    angles = residue.astype(jnp.float32) * (two_pi / period.astype(jnp.float32))
    code = jnp.where(lanes < NF, jnp.sin(angles), jnp.where(lanes < 2 * NF, jnp.cos(angles), 0.0))
    wide = embedding[...].astype(jnp.float32)
    features = jnp.concatenate((wide[:, :LANES] + code, wide[:, LANES:]), axis=1).astype(jnp.bfloat16)
    terms = lax.dot_general(
        features,
        weights[...].astype(jnp.bfloat16),
        (((1,), (1,)), ((), ())),
        preferred_element_type=jnp.float32,
    )
    odd = lanes // own % 2 == 1
    tile[...] = jnp.where(odd, terms[rows // 2 :], terms[: rows // 2])


def chunk_kernel(
    tile_at, ahead_1_at, ahead_2_at, edge_at, conv_bias_at, bias_at, near_at, far_at,
    chunks, last_slab, tile, ahead_1, ahead_2, edge, conv_bias, bias, near_weight, far_weight, sems,
):
    fetch(
        sems, (tile_at, tile), (ahead_1_at, ahead_1), (ahead_2_at, ahead_2), (edge_at, edge),
        (conv_bias_at, conv_bias), (bias_at, bias), (near_at, near_weight), (far_at, far_weight),
    )
    lanes = lane_ids()
    members = chunks.shape[0]
    own, width = bias.shape
    wide = 2 * own
    rows = 2 * tile.shape[0]
    _, member, chan = position(rows, members)
    features = near_weight.shape[1]
    turn = lax.rem(2 * features - (1 - chan) * (features // 2) - member * rows, features)
    near_piece, far_piece = (
        pltpu.roll(w[...].astype(jnp.float32), turn, 1)[:, :LANES] for w in (near_weight, far_weight)
    )
    weight = []
    for j in range(3):
        part = slice(8 * j, 8 * (j + 1))
        both = jnp.where(lanes < rows, near_piece[part], pltpu.roll(far_piece[part], rows, 1))
        weight.append(pltpu.roll(both, 3 * SPARE, 1))
    last_slab[...] = jnp.where(lanes >= 3 * SPARE, weight[2], 0.0)
    piece = pltpu.roll(bias[...], lax.rem(width - member * SPARE, width), 1)[:, :LANES]
    conv_column = column(conv_bias[0:1])
    third = jnp.zeros((8, LANES), jnp.float32)
    for j in range(own // 8):
        part = slice(8 * j, 8 * (j + 1))
        third = jnp.where(lanes // SPARE == j, pltpu.roll(piece[part], j * SPARE, 1), third)
        third = jnp.where(lanes == own // 8 * SPARE + j, conv_column[part], third)
    held = [edge[...], tile[...], ahead_1[...], ahead_2[...], edge[...]]
    first = [pltpu.roll(block, LANES - wide, 1) for block in held]
    near = [pltpu.roll(block, wide, 1) for block in held[:3]]
    one = [jnp.where(lanes < wide, first[k], jnp.where(lanes < 2 * wide, held[k + 1], weight[0])) for k in range(3)]
    for to in range(members):
        before = (member == members - 1) & (to == 0)
        after_last = (member == 0) & (to == members - 1)
        start = jnp.where(before, 0, jnp.where(member < to - 1, 2, 1))

        def chosen(blocks):
            return jnp.where(start == 0, blocks[0], jnp.where(start == 1, blocks[1], blocks[2]))

        near_to = jnp.where(before, near[0], jnp.where(after_last, near[2], near[1]))
        two = jnp.where(lanes < wide, chosen(first[2:]), jnp.where(lanes < 2 * wide, near_to, weight[1]))
        one_to = chosen(one)
        for c in range(2):
            chunks[to, c, 0] = one_to
            chunks[to, c, 1] = two
            chunks[to, c, 2] = third


def last_kernel(
    part_at, ahead_1_at, ahead_2_at, terms_at, recv_at, near_at, far_at,
    out, part, ahead_1, ahead_2, terms, recv, near_here, far_here, blocks, weights, sems,
):
    fetch(
        sems, (part_at, part), (ahead_1_at, ahead_1), (ahead_2_at, ahead_2), (terms_at, terms),
        (recv_at, recv), (near_at, near_here), (far_at, far_here),
    )
    lanes = lane_ids()
    own, features = near_here.shape
    half = features // 2
    wide = 2 * own
    members = terms.shape[0]
    rows = out.shape[0]
    _, _, chan = position(rows, members)
    for k, here in enumerate((far_here, near_here)):
        values = here[...].astype(jnp.float32)
        blocks[0, k * own : (k + 1) * own] = jnp.where(chan == 0, values[:, :half], values[:, half:])
    per_tile = LANES // rows
    for j in range(own // 8):
        for at in range(0, members, per_tile):
            far = near = jnp.zeros((8, LANES), jnp.float32)
            for t in range(min(per_tile, members - at)):
                tile = recv[at + t, 1 - chan].astype(jnp.float32)[: rows // 2] if j == 2 else terms[at + t, 1 - chan, j]
                mine = lanes // rows == t
                near = jnp.where(mine, pltpu.roll(tile, (SPARE + t * rows) % LANES, 1), near)
                far = jnp.where(mine, pltpu.roll(tile, (SPARE - rows + t * rows) % LANES, 1), far)
            span = slice(at * rows, min(at * rows + LANES, half))
            blocks[1, 8 * j : 8 * (j + 1), span] = far[:, : span.stop - span.start]
            blocks[1, own + 8 * j : own + 8 * (j + 1), span] = near[:, : span.stop - span.start]
    total = jnp.zeros((rows // 2, 2 * half), jnp.float32)
    weights[...] = jnp.zeros_like(weights)
    for k, c in enumerate((chan, 1 - chan)):
        for n in range(2):
            block = blocks[k, n * own : (n + 1) * own]
            weights[2 * n * own : (2 * n + 1) * own, :half] = block
            weights[(2 * n + 1) * own : (2 * n + 2) * own, half:] = block
        far = part[c, 0] + pltpu.roll(ahead_1[c], LANES - wide, 1) + ahead_2[c]
        sums = jnp.where(lanes < wide, far, jnp.where(lanes < 2 * wide, part[c, 1], 0.0))
        total += jnp.dot(
            sums.astype(jnp.bfloat16),
            weights[...].astype(jnp.bfloat16),
            preferred_element_type=jnp.float32,
        )
    out[...] = jnp.concatenate((total[:, :half], total[:, half:]), axis=0).astype(out.dtype)


def taps_kernel(conv_weight_at, ahead, back, conv_weight, ahead_wide, back_wide, sems):
    fetch(sems, (conv_weight_at, conv_weight))
    chans = conv_weight.shape[2]
    own = chans // 2
    chan = lax.axis_index("chan")
    ids = [lax.broadcasted_iota(jnp.int32, (chans, chans), k) for k in range(2)]
    turn = (lax.rem(ids[0] + chan * own, chans) == ids[1]).astype(jnp.bfloat16)

    def product(left, right, right_axis):
        dims = (((1,), (right_axis,)), ((), ()))
        return lax.dot_general(left, right, dims, preferred_element_type=jnp.float32)

    for wide in (ahead_wide, back_wide):
        wide[...] = jnp.zeros_like(wide)
    for layer in range(2):
        for tap in range(9):
            step, side = tap // 3 - 1, tap % 3 - 1
            for wide, sign in ((ahead_wide, 1), (back_wide, -1)):
                turned = product(turn, conv_weight[layer, tap], 0 if sign > 0 else 1)
                turned = product(turned.astype(jnp.bfloat16), turn, 1)
                a, m = sign * step, sign * (side - step)
                last = (layer == 1) == (sign > 0)
                count = own if last else chans
                row = (5 * chans if last else 0) + (m + 2) * count
                wide[row : row + count, (a + 1) * chans : (a + 2) * chans] = turned[:count]
    ahead[...] = ahead_wide[...].astype(jnp.bfloat16)
    back[...] = back_wide[...].astype(jnp.bfloat16)


def forward_kernel(
    total_rows, steps, band, terms_at, conv_bias_at, bias_at, taps_at,
    pair_out, slope_0, slope_1, pair_0, act_0, act_1, pair_1, far_rows, near_rows, far, near, bias,
    conv_bias, terms, taps, sems,
):
    band_width, step_0, step_1 = band[0], steps[0], steps[1]
    lanes = lane_ids()
    rows, own, width = pair_out.shape
    first_row, member, chan = position(rows, terms.shape[0])
    chans = 2 * own
    count = width // LANES
    members = terms.shape[0]
    taps_0, taps_1 = taps.at[: 5 * chans], taps.at[5 * chans :]
    fetch(
        sems, (conv_bias_at, conv_bias), (terms_at, terms), (bias_at, bias.at[:own]), (taps_at, taps)
    )
    slabs = own // 8

    lay_slabs(bias, own, [[(terms[k, 1 - chan, 2], j) for k in range(members)] for j in range(slabs)])
    last = terms[0, 1 - chan, 2]
    bias_0 = jnp.concatenate(
        [column(conv_bias[0:1])] + [last[:, k : k + 1] for k in range(slabs * SPARE, slabs * SPARE + slabs)], axis=0
    )
    bias_1 = column(conv_bias[1:2])

    far_rows[...] = jnp.zeros_like(far_rows)
    near_rows[...] = jnp.zeros_like(near_rows)
    half = rows // 2

    def lay_rows(target, place, source, tile, first):
        here, other = terms[source, chan, tile], terms[source, 1 - chan, tile]
        for h in range(2):
            from_lane = first + h * own
            joined = jnp.where(
                lanes < own,
                pltpu.roll(here, (LANES - from_lane) % LANES, 1),
                pltpu.roll(other, (LANES + own - from_lane) % LANES, 1),
            )
            target[place * rows + h * half : place * rows + (h + 1) * half] = joined

    for place in range(width // rows + 3):
        source = lax.rem(member + (members - 1 + place), members)
        j = place // members
        lay_rows(far_rows, place, source, j // 2, j % 2 * 2 * own)
        if place < 3:
            lay_rows(near_rows, place, source, 1, 2 * own)
    for k in range(count + 1):
        span = slice(k * LANES, (k + 1) * LANES)
        far[:, span] = far_rows[span].T[:chans]
    near[...] = near_rows[...].T[:chans]

    def keeps(row):
        limit = limit_of(row, first_row, band_width, total_rows)
        return [lanes + k * LANES < limit for k in range(count)]

    def seed(row, with_slope):
        near_col = pltpu.roll(near[...], lax.rem(LANES - row, LANES), 1)[:, 0:1]
        ahead = pull(tiles_of(far[...]), row, count, lanes)
        for k, keep in enumerate(keeps(row)):
            span = pl.ds(k * LANES, LANES)
            value = jnp.where(keep, near_col + ahead[k] + bias[:, span], 0.0)
            cdf = gelu_cdf(value)
            pair_0[row, :, span] = value
            act_0[row, :, span] = (value * cdf).astype(jnp.bfloat16)
            if with_slope:
                slope_0[row - HALO, :, span] = gelu_slope(value[:own], cdf[:own])

    def outer_seeds(block, _):
        for g in range(SEEDS):
            index = block * SEEDS + g
            seed(jnp.where(index < HALO, index, index + rows), False)
        return 0

    def inner_seeds(block, _):
        for g in range(SEEDS):
            seed(block * SEEDS + g + HALO, True)
        return 0

    lax.fori_loop(0, 2 * HALO // SEEDS, outer_seeds, 0)
    lax.fori_loop(0, rows // SEEDS, inner_seeds, 0)

    def layer_0(block, _):
        first = block * GROUP
        convs = tap_sums(taps_0, act_0, first + DMAX, step_0, chans, lanes)
        for g, conv in enumerate(convs):
            index = first + g
            row = index + DMAX
            for k, keep in enumerate(keeps(row)):
                span = pl.ds(k * LANES, LANES)
                value = jnp.where(keep, pair_0[row, :, span] + conv[k] + bias_0, 0.0)
                cdf = gelu_cdf(value)
                pair_1[index, :, span] = value[:own]
                act_1[index, :, span] = (value * cdf).astype(jnp.bfloat16)
                slope_1[index, :, span] = gelu_slope(value, cdf)
        return 0

    lax.fori_loop(0, (rows + HALO) // GROUP, layer_0, 0)

    def layer_1(block, _):
        first = block * GROUP
        convs = tap_sums(taps_1, act_1, first + DMAX, step_1, own, lanes)
        for g, conv in enumerate(convs):
            index = first + g
            for k, keep in enumerate(keeps(index + HALO)):
                span = pl.ds(k * LANES, LANES)
                value = jnp.where(keep, pair_1[index + DMAX, :, span] + conv[k] + bias_1, 0.0)
                pair_out[index, :, span] = value
        return 0

    lax.fori_loop(0, rows // GROUP, layer_1, 0)


def backward_kernel(
    total_rows, steps, band, slope_0, slope_1, cot_behind, cot_here, cot_ahead, last_slab_at, taps_at,
    far_terms, grad_2, grad_1, low_1, near_sum, far_sum, far_rows, taps, last_slab, sems,
):
    band_width, step_0, step_1 = band[0], steps[0], steps[1]
    lanes = lane_ids()
    rows, chans, width = cot_here.shape
    first_row, member, _ = position(rows, far_terms.shape[0])
    own = chans // 2
    count = width // LANES
    members = far_terms.shape[0]
    taps_1, taps_0 = taps.at[: 5 * chans], taps.at[5 * chans :]

    def keeps(row):
        limit = limit_of(row, first_row, band_width, total_rows)
        return [lanes + k * LANES < limit for k in range(count)]

    fetch(
        sems,
        (cot_behind, grad_2.at[:rows]),
        (cot_here, grad_2.at[rows : 2 * rows]),
        (cot_ahead, grad_2.at[2 * rows :]),
        (taps_at, taps),
        (last_slab_at, last_slab),
    )

    def layer_1(block, _):
        first = block * GROUP
        convs = tap_sums(taps_1, grad_2, first + DMAX, step_1, chans, lanes)
        for g, conv in enumerate(convs):
            index = first + g
            row = index + DMAX
            for k, keep in enumerate(keeps(row)):
                span = pl.ds(k * LANES, LANES)
                above = grad_2[row, :, span].astype(jnp.float32)
                value = jnp.where(keep, above + slope_1[index, :, span] * conv[k], 0.0)
                grad_1[index, :, span] = value[:own]
                low_1[index, :, span] = value.astype(jnp.bfloat16)
        return 0

    lax.fori_loop(0, (rows + HALO) // GROUP, layer_1, 0)

    near_sum[...] = jnp.zeros_like(near_sum)
    far_sum[...] = jnp.zeros_like(far_sum)

    def layer_0(block, _):
        first = block * GROUP
        convs = tap_sums(taps_0, low_1, first + DMAX, step_0, own, lanes)
        for g, conv in enumerate(convs):
            index = first + g
            values = []
            for k, keep in enumerate(keeps(index + HALO)):
                span = pl.ds(k * LANES, LANES)
                above = grad_1[index + DMAX, :, span]
                values.append(jnp.where(keep, above + slope_0[index, :, span] * conv[k], 0.0))
            total = jnp.sum(sum(values[1:], values[0]), axis=1, keepdims=True)
            near_sum[:own] += jnp.where(lanes == index, total, 0.0)
            for k, tile in enumerate(push(values, index, count + 1, lanes)):
                far_sum[:own, k * LANES : (k + 1) * LANES] += tile
        return 0

    lax.fori_loop(0, rows // GROUP, layer_0, 0)

    far_rows[...] = jnp.zeros_like(far_rows)
    for k in range(count + 1):
        start = pl.multiple_of(member * rows, 8) + k * LANES
        far_rows[pl.ds(start, LANES)] = far_sum[:, k * LANES : (k + 1) * LANES].T
    half = rows // 2
    near_rows = near_sum[...].T
    near_terms = pltpu.roll(near_rows[:half], 2 * own, 1) + pltpu.roll(near_rows[half:rows], 3 * own, 1)

    def halves(slot):
        return [far_rows[slot * rows + h * half : slot * rows + (h + 1) * half] for h in range(2)]

    for r in range(members):
        pieces = halves(r) + halves(members + r)
        one = sum([pltpu.roll(piece, k * own, 1) for k, piece in enumerate(pieces) if k], pieces[0])
        one = one + last_slab[...]
        pieces = halves(2 * members + r)
        own_place = jnp.where(member == r, near_terms, 0.0)
        two = pieces[0] + pltpu.roll(pieces[1], own, 1) + own_place
        both = jnp.concatenate((one, two), axis=0).astype(far_terms.dtype)
        for c in range(2):
            far_terms[r, c] = both


def call(
    kernel, out_shapes, scratch, flops, scalars, near_arrays, far_arrays=(), stored_arrays=(), grant=32
):
    arrays = tuple(near_arrays) + tuple(far_arrays) + tuple(stored_arrays)
    bytes_accessed = sum(a.size * a.dtype.itemsize for a in arrays)
    bytes_accessed += sum(s.size * s.dtype.itemsize for s in out_shapes)
    vmem = pl.BlockSpec(memory_space=pltpu.VMEM)
    return pl.pallas_call(
        kernel,
        out_shape=out_shapes,
        in_specs=[pl.BlockSpec(memory_space=pltpu.SMEM)] * len(scalars)
        + [vmem] * len(near_arrays)
        + [pl.BlockSpec(memory_space=pl.ANY)] * len(far_arrays)
        + [pl.BlockSpec(memory_space=pltpu.HBM)] * len(stored_arrays),
        out_specs=[vmem] * len(out_shapes),
        scratch_shapes=scratch,
        compiler_params=pltpu.CompilerParams(vmem_limit_bytes=grant * 2**20),
        cost_estimate=pl.CostEstimate(
            flops=flops, bytes_accessed=bytes_accessed, transcendentals=0
        ),
    )(*scalars, *arrays)


f32 = functools.partial(jax.ShapeDtypeStruct, dtype=jnp.float32)


def fetching_call(kernel, out_shapes, scratch, scalars, far_arrays, stored_arrays, grant=32):
    arrays = tuple(far_arrays) + tuple(stored_arrays)
    held = [pltpu.VMEM(a.shape, a.dtype) for a in arrays]
    sems = pltpu.SemaphoreType.DMA((len(arrays),))
    return call(
        kernel, out_shapes, held + scratch + [sems], 0, scalars, (), far_arrays, stored_arrays, grant
    )


def tile_call(scalars, embedding, near_weight, far_weight):
    shape = (embedding.shape[0] // 2, LANES)
    weights = pltpu.VMEM((LANES, embedding.shape[1]), jnp.float32)
    (tile,) = fetching_call(
        tile_kernel, (f32(shape),), [weights], scalars, (), (embedding, near_weight, far_weight), GRANT
    )
    return tile


def taps_call(conv_weight):
    chans = conv_weight.shape[2]
    shape = (-(-(5 * chans + 5 * chans // 2) // 16) * 16, 3 * chans)
    return fetching_call(
        taps_kernel,
        (jax.ShapeDtypeStruct(shape, jnp.bfloat16),) * 2,
        [pltpu.VMEM(shape, jnp.float32)] * 2,
        (),
        (),
        (conv_weight,),
    )


def chunk_call(members, tiles, *arrays):
    shape = tiles[0].shape
    return fetching_call(chunk_kernel, (f32((members, 2, 3) + shape), f32(shape)), [], (), tiles, arrays, GRANT)


def last_call(part, ahead_1, ahead_2, terms, recv, near_weight, far_weight):
    own, features = near_weight.shape
    (out,) = fetching_call(
        last_kernel,
        (jax.ShapeDtypeStruct((2 * part.shape[2], features // 2), jnp.bfloat16),),
        [
            pltpu.VMEM((2, 2 * own, features // 2), jnp.float32),
            pltpu.VMEM((LANES, features), jnp.float32),
        ],
        (),
        (part, ahead_1, ahead_2, terms, recv),
        (near_weight, far_weight),
    )
    return out


def forward_call(total_rows, rows, scalars, terms, bias_here, conv_bias, taps):
    own, width = bias_here.shape
    chans = 2 * own
    return call(
        functools.partial(forward_kernel, total_rows),
        (f32((rows, own, width)), f32((rows, own, width)), f32((rows + HALO, chans, width))),
        [
            pltpu.VMEM((rows + 2 * HALO, chans, width), jnp.float32),
            pltpu.VMEM((rows + 2 * HALO, chans, width), jnp.bfloat16),
            pltpu.VMEM((rows + HALO, chans, width), jnp.bfloat16),
            pltpu.VMEM((rows + HALO, own, width), jnp.float32),
            pltpu.VMEM((width + LANES, LANES), jnp.float32),
            pltpu.VMEM((LANES, LANES), jnp.float32),
            pltpu.VMEM((chans, width + LANES), jnp.float32),
            pltpu.VMEM((chans, LANES), jnp.float32),
            pltpu.VMEM((chans, width), jnp.float32),
            pltpu.VMEM(conv_bias.shape, conv_bias.dtype),
            pltpu.VMEM(terms.shape, terms.dtype),
            pltpu.VMEM(taps.shape, taps.dtype),
            pltpu.SemaphoreType.DMA((4,)),
        ],
        2 * 15 * chans * chans * width * 40,
        scalars,
        (),
        (terms,),
        (conv_bias, bias_here, taps),
    )


def backward_call(total_rows, members, scalars, cot_behind, cot, cot_ahead, slope_0, slope_1, last_slab, taps):
    rows, chans, width = cot.shape
    own = chans // 2
    slots = members + (width + LANES) // rows
    (terms,) = call(
        functools.partial(backward_kernel, total_rows),
        (jax.ShapeDtypeStruct((members, 2, rows, LANES), jnp.bfloat16),),
        [
            pltpu.VMEM((rows + 2 * HALO, chans, width), jnp.bfloat16),
            pltpu.VMEM((rows + HALO, own, width), jnp.float32),
            pltpu.VMEM((rows + HALO, chans, width), jnp.bfloat16),
            pltpu.VMEM((LANES, LANES), jnp.float32),
            pltpu.VMEM((LANES, width + LANES), jnp.float32),
            pltpu.VMEM((slots * rows, LANES), jnp.float32),
            pltpu.VMEM(taps.shape, taps.dtype),
            pltpu.VMEM(last_slab.shape, last_slab.dtype),
            pltpu.SemaphoreType.DMA((5,)),
        ],
        2 * 15 * chans * chans * width * 40,
        scalars,
        (slope_0, slope_1),
        (cot_behind, cot, cot_ahead, last_slab),
        (taps,),
    )
    return terms


def exchange_in_group(chunks):
    members = chunks.shape[0]
    lists = [
        [2 * (q * members + k) + c for k in range(members) for c in range(2)]
        for q in range(lax.axis_size("chrom") // members)
    ]
    flat = chunks.reshape((2 * members,) + chunks.shape[2:])
    recv = lax.all_to_all(flat, ("chrom", "chan"), 0, 0, axis_index_groups=lists)
    return recv.reshape(chunks.shape)


def from_edges(block, members):
    count = lax.axis_size("chrom")
    route = [(i + 3 * members, i) for i in range(0, count - 3 * members, members)]
    route += [(i - members, i) for i in range(2 * members - 1, count, members)]
    return lax.ppermute(block, "chrom", route)


def shards(
    embedding, window_start, band_width, dilations, near_weight, far_weight,
    distance_bias, conv_weight, conv_bias, cotangent,
):
    rows = embedding.shape[0]
    own, width = distance_bias.shape
    chans = conv_weight.shape[2]
    features_half = embedding.shape[1] // 2
    chan = lax.axis_index("chan")
    place = lax.axis_index("chrom")
    first_row = place * rows
    total_rows = lax.axis_size("chrom") * rows
    members = width // rows // 2
    member = place % members
    row_ids = first_row + jnp.arange(rows, dtype=jnp.int32)
    scalars = (dilations, band_width)

    near_weight, far_weight = near_weight.T, far_weight.T
    tile = tile_call((window_start,), embedding, near_weight, far_weight)
    ahead = from_ahead(tile, members), from_ahead(tile, 2 * members), from_edges(tile, members)

    chunks, last_slab = chunk_call(
        members, (tile,) + ahead, conv_bias, distance_bias, near_weight, far_weight
    )
    terms = exchange_in_group(chunks)

    cot_other = from_partner(cotangent)
    offsets = jnp.arange(width, dtype=jnp.int32)
    keep = (offsets[None, :] < band_width[0]) & (row_ids[:, None] + offsets[None, :] < total_rows)
    cot = jnp.concatenate((cotangent, after(cot_other, chunks)), axis=0)
    cot = jnp.where(keep[:, None, :], jnp.swapaxes(cot, 0, 1), 0).astype(jnp.bfloat16)
    cot_behind = from_ahead(cot, -1)
    cot_ahead = from_ahead(cot, 1)

    taps_ahead, taps_back = taps_call(after(conv_weight, chunks))
    pair_rows, slope_0, slope_1 = forward_call(
        total_rows, rows, scalars, terms, distance_bias, conv_bias, taps_ahead
    )
    pair_out = jnp.swapaxes(pair_rows.astype(jnp.bfloat16), 0, 1)
    terms_back = backward_call(
        total_rows, members, scalars, cot_behind, cot, cot_ahead, slope_0, slope_1, last_slab, taps_back
    )
    recv = exchange_in_group(terms_back)
    part = jnp.sum(recv.astype(jnp.float32), axis=0).reshape(2, 2, rows // 2, LANES)
    ahead_1 = from_ahead(part[:, 0], -members)
    ahead_2 = from_ahead(part[:, 1], -2 * members)
    grads = last_call(part, ahead_1, ahead_2, terms, recv, near_weight, far_weight)
    return (pair_out, grads)


def solution(mesh):
    in_specs = (
        P("chrom", None),
        P(),
        P(),
        P(),
        P(None, "chan"),
        P(None, "chan"),
        P("chan", None),
        P(),
        P(None, "chan"),
        P("chan", "chrom", None),
    )
    out_specs = (P("chan", "chrom", None), P("chrom", "chan"))
    return jax.shard_map(shards, mesh=mesh, in_specs=in_specs, out_specs=out_specs, check_vma=False)
```

```python
import functools

import jax
import jax.numpy as jnp
from jax import lax
from jax.experimental import pallas as pl
from jax.experimental.pallas import tpu as pltpu
from jax.sharding import PartitionSpec as P

DMAX = 8
NF = 16
HALO = 2 * DMAX
LANES = 128
SPARE = 32
GROUP = 16
GRANT = 60
SEEDS = 8

two_pi = 6.283185307179586
inv_sqrt2 = 0.7071067811865476
inv_sqrt_2pi = 0.3989422804014327


def from_ahead(block, distance):
    devices = range(lax.axis_size("chrom"))
    route = [(i + distance, i) for i in devices if i + distance in devices]
    return lax.ppermute(block, "chrom", route)


def after(block, earlier):
    return lax.optimization_barrier((block, earlier))[0]


def from_partner(block):
    return lax.ppermute(block, "chan", [(0, 1), (1, 0)])


def lane_ids():
    return lax.broadcasted_iota(jnp.int32, (1, LANES), 1)


def tiles_of(values):
    return [values[:, k : k + LANES] for k in range(0, values.shape[1], LANES)]


def pull(tiles, amount, count, lanes):
    turned = [pltpu.roll(tile, lax.rem(LANES - amount, LANES), 1) for tile in tiles]
    turned.append(jnp.zeros_like(turned[0]))
    inside = lanes < LANES - amount
    return [jnp.where(inside, turned[k], turned[k + 1]) for k in range(count)]


def push(tiles, amount, count, lanes):
    zero = jnp.zeros_like(tiles[0])
    turned = [zero] + [pltpu.roll(tile, amount, 1) for tile in tiles] + [zero]
    inside = lanes >= amount
    return [jnp.where(inside, turned[k + 1], turned[k]) for k in range(count)]


def tap_sums(weights, ref, first, dilation, out_count, lanes):
    width = ref.shape[2]
    count = width // LANES
    window = jnp.concatenate(
        [
            jnp.concatenate([ref[first + g + a * dilation] for a in (-1, 0, 1)], axis=0)
            for g in range(GROUP)
        ],
        axis=1,
    )
    stacked = jnp.dot(weights[...], window, preferred_element_type=jnp.float32)
    sums = []
    for g in range(GROUP):
        part = [
            tiles_of(stacked[k * out_count : (k + 1) * out_count, g * width : (g + 1) * width])
            for k in range(5)
        ]
        shifted = [
            push(part[0], 2 * dilation, count, lanes),
            push(part[1], dilation, count, lanes),
            part[2],
            pull(part[3], dilation, count, lanes),
            pull(part[4], 2 * dilation, count, lanes),
        ]
        sums.append([sum(tile[1:], tile[0]) for tile in zip(*shifted)])
    return sums


def limit_of(row, first_row, band_width, total_rows):
    here = first_row - HALO + row
    return jnp.where(here < 0, 0, jnp.minimum(band_width, total_rows - here))


def gelu_cdf(values):
    return 0.5 + 0.5 * lax.erf(values * inv_sqrt2)


def gelu_slope(values, cdf):
    return cdf + values * (inv_sqrt_2pi * jnp.exp(-0.5 * values * values))


def position(rows, members):
    place = lax.axis_index("chrom")
    return place * rows, lax.rem(place, members), lax.axis_index("chan")


def column(row):
    count = row.shape[1]
    same = [lax.broadcasted_iota(jnp.int32, (count, count), k) for k in range(2)]
    return jnp.sum(jnp.where(same[0] == same[1], row, 0.0), axis=1, keepdims=True)


def fetch(sems, *pairs):
    copies = [pltpu.make_async_copy(a, b, sems.at[k]) for k, (a, b) in enumerate(pairs)]
    for copy in copies:
        copy.start()
    for copy in copies:
        copy.wait()


def lay_slabs(target, row, slabs):
    lanes = lane_ids()
    per_tile = LANES // SPARE
    for j, pieces in enumerate(slabs):
        for k in range(0, len(pieces), per_tile):
            block = jnp.zeros((8, LANES), jnp.float32)
            for t, (tile, at) in enumerate(pieces[k : k + per_tile]):
                block = jnp.where(lanes // SPARE == t, pltpu.roll(tile, (t - at) % per_tile * SPARE, 1), block)
            target[row + 8 * j : row + 8 * (j + 1), k * SPARE : k * SPARE + LANES] = block


def tile_kernel(start, embedding_at, near_at, far_at, tile, embedding, near, far, weights, sems):
    fetch(sems, (embedding_at, embedding), (near_at, near), (far_at, far))
    rows = embedding.shape[0]
    own = near.shape[0]
    weights[...] = jnp.zeros_like(weights)
    for k, part in enumerate((near, near, far, far)):
        weights[k * own : (k + 1) * own] = part[...].astype(jnp.float32)
    lanes = lane_ids()
    first_row = lax.axis_index("chrom") * rows
    row_ids = start[0] + first_row + lax.broadcasted_iota(jnp.int32, (rows, LANES), 0)
    octave = lax.broadcasted_iota(jnp.int32, (rows, LANES), 1) % NF
    period = lax.shift_left(jnp.ones_like(octave), octave + 2)
    residue = row_ids & (period - 1)
    angles = residue.astype(jnp.float32) * (two_pi / period.astype(jnp.float32))
    code = jnp.where(lanes < NF, jnp.sin(angles), jnp.where(lanes < 2 * NF, jnp.cos(angles), 0.0))
    wide = embedding[...].astype(jnp.float32)
    features = jnp.concatenate((wide[:, :LANES] + code, wide[:, LANES:]), axis=1).astype(jnp.bfloat16)
    terms = lax.dot_general(
        features,
        weights[...].astype(jnp.bfloat16),
        (((1,), (1,)), ((), ())),
        preferred_element_type=jnp.float32,
    )
    odd = lanes // own % 2 == 1
    tile[...] = jnp.where(odd, terms[rows // 2 :], terms[: rows // 2])


def chunk_kernel(
    tile_at, ahead_1_at, ahead_2_at, edge_at, conv_bias_at, bias_at, near_at, far_at,
    chunks, last_slab, tile, ahead_1, ahead_2, edge, conv_bias, bias, near_weight, far_weight, sems,
):
    fetch(
        sems, (tile_at, tile), (ahead_1_at, ahead_1), (ahead_2_at, ahead_2), (edge_at, edge),
        (conv_bias_at, conv_bias), (bias_at, bias), (near_at, near_weight), (far_at, far_weight),
    )
    lanes = lane_ids()
    members = chunks.shape[0]
    own, width = bias.shape
    wide = 2 * own
    rows = 2 * tile.shape[0]
    _, member, chan = position(rows, members)
    features = near_weight.shape[1]
    turn = lax.rem(2 * features - (1 - chan) * (features // 2) - member * rows, features)
    near_piece, far_piece = (
        pltpu.roll(w[...].astype(jnp.float32), turn, 1)[:, :LANES] for w in (near_weight, far_weight)
    )
    weight = []
    for j in range(3):
        part = slice(8 * j, 8 * (j + 1))
        both = jnp.where(lanes < rows, near_piece[part], pltpu.roll(far_piece[part], rows, 1))
        weight.append(pltpu.roll(both, 3 * SPARE, 1))
    last_slab[...] = jnp.where(lanes >= 3 * SPARE, weight[2], 0.0)
    piece = pltpu.roll(bias[...], lax.rem(width - member * SPARE, width), 1)[:, :LANES]
    conv_column = column(conv_bias[0:1])
    third = jnp.zeros((8, LANES), jnp.float32)
    for j in range(own // 8):
        part = slice(8 * j, 8 * (j + 1))
        third = jnp.where(lanes // SPARE == j, pltpu.roll(piece[part], j * SPARE, 1), third)
        third = jnp.where(lanes == own // 8 * SPARE + j, conv_column[part], third)
    held = [edge[...], tile[...], ahead_1[...], ahead_2[...], edge[...]]
    first = [pltpu.roll(block, LANES - wide, 1) for block in held]
    near = [pltpu.roll(block, wide, 1) for block in held[:3]]
    one = [jnp.where(lanes < wide, first[k], jnp.where(lanes < 2 * wide, held[k + 1], weight[0])) for k in range(3)]
    for to in range(members):
        before = (member == members - 1) & (to == 0)
        after_last = (member == 0) & (to == members - 1)
        start = jnp.where(before, 0, jnp.where(member < to - 1, 2, 1))

        def chosen(blocks):
            return jnp.where(start == 0, blocks[0], jnp.where(start == 1, blocks[1], blocks[2]))

        near_to = jnp.where(before, near[0], jnp.where(after_last, near[2], near[1]))
        two = jnp.where(lanes < wide, chosen(first[2:]), jnp.where(lanes < 2 * wide, near_to, weight[1]))
        one_to = chosen(one)
        for c in range(2):
            chunks[to, c, 0] = one_to
            chunks[to, c, 1] = two
            chunks[to, c, 2] = third


def last_kernel(
    part_at, ahead_1_at, ahead_2_at, terms_at, recv_at, near_at, far_at,
    out, part, ahead_1, ahead_2, terms, recv, near_here, far_here, blocks, weights, sems,
):
    fetch(
        sems, (part_at, part), (ahead_1_at, ahead_1), (ahead_2_at, ahead_2), (terms_at, terms),
        (recv_at, recv), (near_at, near_here), (far_at, far_here),
    )
    lanes = lane_ids()
    own, features = near_here.shape
    half = features // 2
    wide = 2 * own
    members = terms.shape[0]
    rows = out.shape[0]
    _, _, chan = position(rows, members)
    for k, here in enumerate((far_here, near_here)):
        values = here[...].astype(jnp.float32)
        blocks[0, k * own : (k + 1) * own] = jnp.where(chan == 0, values[:, :half], values[:, half:])
    per_tile = LANES // rows
    for j in range(own // 8):
        for at in range(0, members, per_tile):
            far = near = jnp.zeros((8, LANES), jnp.float32)
            for t in range(min(per_tile, members - at)):
                tile = recv[at + t, 1 - chan].astype(jnp.float32)[: rows // 2] if j == 2 else terms[at + t, 1 - chan, j]
                mine = lanes // rows == t
                near = jnp.where(mine, pltpu.roll(tile, (SPARE + t * rows) % LANES, 1), near)
                far = jnp.where(mine, pltpu.roll(tile, (SPARE - rows + t * rows) % LANES, 1), far)
            span = slice(at * rows, min(at * rows + LANES, half))
            blocks[1, 8 * j : 8 * (j + 1), span] = far[:, : span.stop - span.start]
            blocks[1, own + 8 * j : own + 8 * (j + 1), span] = near[:, : span.stop - span.start]
    total = jnp.zeros((rows // 2, 2 * half), jnp.float32)
    weights[...] = jnp.zeros_like(weights)
    for k, c in enumerate((chan, 1 - chan)):
        for n in range(2):
            block = blocks[k, n * own : (n + 1) * own]
            weights[2 * n * own : (2 * n + 1) * own, :half] = block
            weights[(2 * n + 1) * own : (2 * n + 2) * own, half:] = block
        far = part[c, 0] + pltpu.roll(ahead_1[c], LANES - wide, 1) + ahead_2[c]
        sums = jnp.where(lanes < wide, far, jnp.where(lanes < 2 * wide, part[c, 1], 0.0))
        total += jnp.dot(
            sums.astype(jnp.bfloat16),
            weights[...].astype(jnp.bfloat16),
            preferred_element_type=jnp.float32,
        )
    out[...] = jnp.concatenate((total[:, :half], total[:, half:]), axis=0).astype(out.dtype)


def taps_kernel(conv_weight_at, ahead, back, conv_weight, ahead_wide, back_wide, sems):
    fetch(sems, (conv_weight_at, conv_weight))
    chans = conv_weight.shape[2]
    own = chans // 2
    chan = lax.axis_index("chan")
    ids = [lax.broadcasted_iota(jnp.int32, (chans, chans), k) for k in range(2)]
    turn = (lax.rem(ids[0] + chan * own, chans) == ids[1]).astype(jnp.bfloat16)

    def product(left, right, right_axis):
        dims = (((1,), (right_axis,)), ((), ()))
        return lax.dot_general(left, right, dims, preferred_element_type=jnp.float32)

    for wide in (ahead_wide, back_wide):
        wide[...] = jnp.zeros_like(wide)
    for layer in range(2):
        for tap in range(9):
            step, side = tap // 3 - 1, tap % 3 - 1
            for wide, sign in ((ahead_wide, 1), (back_wide, -1)):
                turned = product(turn, conv_weight[layer, tap], 0 if sign > 0 else 1)
                turned = product(turned.astype(jnp.bfloat16), turn, 1)
                a, m = sign * step, sign * (side - step)
                last = (layer == 1) == (sign > 0)
                count = own if last else chans
                row = (5 * chans if last else 0) + (m + 2) * count
                wide[row : row + count, (a + 1) * chans : (a + 2) * chans] = turned[:count]
    ahead[...] = ahead_wide[...].astype(jnp.bfloat16)
    back[...] = back_wide[...].astype(jnp.bfloat16)


def forward_kernel(
    total_rows, steps, band, terms_at, conv_bias_at, bias_at, taps_at,
    pair_out, slope_0, slope_1, pair_0, act_0, act_1, pair_1, far_rows, near_rows, far, near, bias,
    conv_bias, terms, taps, sems,
):
    band_width, step_0, step_1 = band[0], steps[0], steps[1]
    lanes = lane_ids()
    rows, own, width = pair_out.shape
    first_row, member, chan = position(rows, terms.shape[0])
    chans = 2 * own
    count = width // LANES
    members = terms.shape[0]
    taps_0, taps_1 = taps.at[: 5 * chans], taps.at[5 * chans :]
    fetch(
        sems, (conv_bias_at, conv_bias), (terms_at, terms), (bias_at, bias.at[:own]), (taps_at, taps)
    )
    slabs = own // 8

    lay_slabs(bias, own, [[(terms[k, 1 - chan, 2], j) for k in range(members)] for j in range(slabs)])
    last = terms[0, 1 - chan, 2]
    bias_0 = jnp.concatenate(
        [column(conv_bias[0:1])] + [last[:, k : k + 1] for k in range(slabs * SPARE, slabs * SPARE + slabs)], axis=0
    )
    bias_1 = column(conv_bias[1:2])

    far_rows[...] = jnp.zeros_like(far_rows)
    near_rows[...] = jnp.zeros_like(near_rows)
    half = rows // 2

    def lay_rows(target, place, source, tile, first):
        here, other = terms[source, chan, tile], terms[source, 1 - chan, tile]
        for h in range(2):
            from_lane = first + h * own
            joined = jnp.where(
                lanes < own,
                pltpu.roll(here, (LANES - from_lane) % LANES, 1),
                pltpu.roll(other, (LANES + own - from_lane) % LANES, 1),
            )
            target[place * rows + h * half : place * rows + (h + 1) * half] = joined

    for place in range(width // rows + 3):
        source = lax.rem(member + (members - 1 + place), members)
        j = place // members
        lay_rows(far_rows, place, source, j // 2, j % 2 * 2 * own)
        if place < 3:
            lay_rows(near_rows, place, source, 1, 2 * own)
    for k in range(count + 1):
        span = slice(k * LANES, (k + 1) * LANES)
        far[:, span] = far_rows[span].T[:chans]
    near[...] = near_rows[...].T[:chans]

    def keeps(row):
        limit = limit_of(row, first_row, band_width, total_rows)
        return [lanes + k * LANES < limit for k in range(count)]

    def seed(row, with_slope):
        near_col = pltpu.roll(near[...], lax.rem(LANES - row, LANES), 1)[:, 0:1]
        ahead = pull(tiles_of(far[...]), row, count, lanes)
        for k, keep in enumerate(keeps(row)):
            span = pl.ds(k * LANES, LANES)
            value = jnp.where(keep, near_col + ahead[k] + bias[:, span], 0.0)
            cdf = gelu_cdf(value)
            pair_0[row, :, span] = value
            act_0[row, :, span] = (value * cdf).astype(jnp.bfloat16)
            if with_slope:
                slope_0[row - HALO, :, span] = gelu_slope(value[:own], cdf[:own])

    def outer_seeds(block, _):
        for g in range(SEEDS):
            index = block * SEEDS + g
            seed(jnp.where(index < HALO, index, index + rows), False)
        return 0

    def inner_seeds(block, _):
        for g in range(SEEDS):
            seed(block * SEEDS + g + HALO, True)
        return 0

    lax.fori_loop(0, 2 * HALO // SEEDS, outer_seeds, 0)
    lax.fori_loop(0, rows // SEEDS, inner_seeds, 0)

    def layer_0(block, _):
        first = block * GROUP
        convs = tap_sums(taps_0, act_0, first + DMAX, step_0, chans, lanes)
        for g, conv in enumerate(convs):
            index = first + g
            row = index + DMAX
            for k, keep in enumerate(keeps(row)):
                span = pl.ds(k * LANES, LANES)
                value = jnp.where(keep, pair_0[row, :, span] + conv[k] + bias_0, 0.0)
                cdf = gelu_cdf(value)
                pair_1[index, :, span] = value[:own]
                act_1[index, :, span] = (value * cdf).astype(jnp.bfloat16)
                slope_1[index, :, span] = gelu_slope(value, cdf)
        return 0

    lax.fori_loop(0, (rows + HALO) // GROUP, layer_0, 0)

    def layer_1(block, _):
        first = block * GROUP
        convs = tap_sums(taps_1, act_1, first + DMAX, step_1, own, lanes)
        for g, conv in enumerate(convs):
            index = first + g
            for k, keep in enumerate(keeps(index + HALO)):
                span = pl.ds(k * LANES, LANES)
                value = jnp.where(keep, pair_1[index + DMAX, :, span] + conv[k] + bias_1, 0.0)
                pair_out[index, :, span] = value
        return 0

    lax.fori_loop(0, rows // GROUP, layer_1, 0)


def backward_kernel(
    total_rows, steps, band, slope_0, slope_1, cot_behind, cot_here, cot_ahead, last_slab_at, taps_at,
    far_terms, grad_2, grad_1, low_1, near_sum, far_sum, far_rows, taps, last_slab, sems,
):
    band_width, step_0, step_1 = band[0], steps[0], steps[1]
    lanes = lane_ids()
    rows, chans, width = cot_here.shape
    first_row, member, _ = position(rows, far_terms.shape[0])
    own = chans // 2
    count = width // LANES
    members = far_terms.shape[0]
    taps_1, taps_0 = taps.at[: 5 * chans], taps.at[5 * chans :]

    def keeps(row):
        limit = limit_of(row, first_row, band_width, total_rows)
        return [lanes + k * LANES < limit for k in range(count)]

    fetch(
        sems,
        (cot_behind, grad_2.at[:rows]),
        (cot_here, grad_2.at[rows : 2 * rows]),
        (cot_ahead, grad_2.at[2 * rows :]),
        (taps_at, taps),
        (last_slab_at, last_slab),
    )

    def layer_1(block, _):
        first = block * GROUP
        convs = tap_sums(taps_1, grad_2, first + DMAX, step_1, chans, lanes)
        for g, conv in enumerate(convs):
            index = first + g
            row = index + DMAX
            for k, keep in enumerate(keeps(row)):
                span = pl.ds(k * LANES, LANES)
                above = grad_2[row, :, span].astype(jnp.float32)
                value = jnp.where(keep, above + slope_1[index, :, span] * conv[k], 0.0)
                grad_1[index, :, span] = value[:own]
                low_1[index, :, span] = value.astype(jnp.bfloat16)
        return 0

    lax.fori_loop(0, (rows + HALO) // GROUP, layer_1, 0)

    near_sum[...] = jnp.zeros_like(near_sum)
    far_sum[...] = jnp.zeros_like(far_sum)

    def layer_0(block, _):
        first = block * GROUP
        convs = tap_sums(taps_0, low_1, first + DMAX, step_0, own, lanes)
        for g, conv in enumerate(convs):
            index = first + g
            values = []
            for k, keep in enumerate(keeps(index + HALO)):
                span = pl.ds(k * LANES, LANES)
                above = grad_1[index + DMAX, :, span]
                values.append(jnp.where(keep, above + slope_0[index, :, span] * conv[k], 0.0))
            total = jnp.sum(sum(values[1:], values[0]), axis=1, keepdims=True)
            near_sum[:own] += jnp.where(lanes == index, total, 0.0)
            for k, tile in enumerate(push(values, index, count + 1, lanes)):
                far_sum[:own, k * LANES : (k + 1) * LANES] += tile
        return 0

    lax.fori_loop(0, rows // GROUP, layer_0, 0)

    far_rows[...] = jnp.zeros_like(far_rows)
    for k in range(count + 1):
        start = pl.multiple_of(member * rows, 8) + k * LANES
        far_rows[pl.ds(start, LANES)] = far_sum[:, k * LANES : (k + 1) * LANES].T
    half = rows // 2
    near_rows = near_sum[...].T
    near_terms = pltpu.roll(near_rows[:half], 2 * own, 1) + pltpu.roll(near_rows[half:rows], 3 * own, 1)

    def halves(slot):
        return [far_rows[slot * rows + h * half : slot * rows + (h + 1) * half] for h in range(2)]

    for r in range(members):
        pieces = halves(r) + halves(members + r)
        one = sum([pltpu.roll(piece, k * own, 1) for k, piece in enumerate(pieces) if k], pieces[0])
        one = one + last_slab[...]
        pieces = halves(2 * members + r)
        own_place = jnp.where(member == r, near_terms, 0.0)
        two = pieces[0] + pltpu.roll(pieces[1], own, 1) + own_place
        both = jnp.concatenate((one, two), axis=0).astype(far_terms.dtype)
        for c in range(2):
            far_terms[r, c] = both


def call(
    kernel, out_shapes, scratch, flops, scalars, near_arrays, far_arrays=(), stored_arrays=(), grant=32
):
    arrays = tuple(near_arrays) + tuple(far_arrays) + tuple(stored_arrays)
    bytes_accessed = sum(a.size * a.dtype.itemsize for a in arrays)
    bytes_accessed += sum(s.size * s.dtype.itemsize for s in out_shapes)
    vmem = pl.BlockSpec(memory_space=pltpu.VMEM)
    return pl.pallas_call(
        kernel,
        out_shape=out_shapes,
        in_specs=[pl.BlockSpec(memory_space=pltpu.SMEM)] * len(scalars)
        + [vmem] * len(near_arrays)
        + [pl.BlockSpec(memory_space=pl.ANY)] * len(far_arrays)
        + [pl.BlockSpec(memory_space=pltpu.HBM)] * len(stored_arrays),
        out_specs=[vmem] * len(out_shapes),
        scratch_shapes=scratch,
        compiler_params=pltpu.CompilerParams(vmem_limit_bytes=grant * 2**20),
        cost_estimate=pl.CostEstimate(
            flops=flops, bytes_accessed=bytes_accessed, transcendentals=0
        ),
    )(*scalars, *arrays)


f32 = functools.partial(jax.ShapeDtypeStruct, dtype=jnp.float32)


def fetching_call(kernel, out_shapes, scratch, scalars, far_arrays, stored_arrays, grant=32):
    arrays = tuple(far_arrays) + tuple(stored_arrays)
    held = [pltpu.VMEM(a.shape, a.dtype) for a in arrays]
    sems = pltpu.SemaphoreType.DMA((len(arrays),))
    return call(
        kernel, out_shapes, held + scratch + [sems], 0, scalars, (), far_arrays, stored_arrays, grant
    )


def tile_call(scalars, embedding, near_weight, far_weight):
    shape = (embedding.shape[0] // 2, LANES)
    weights = pltpu.VMEM((LANES, embedding.shape[1]), jnp.float32)
    (tile,) = fetching_call(
        tile_kernel, (f32(shape),), [weights], scalars, (), (embedding, near_weight, far_weight), GRANT
    )
    return tile


def taps_call(conv_weight):
    chans = conv_weight.shape[2]
    shape = (-(-(5 * chans + 5 * chans // 2) // 16) * 16, 3 * chans)
    return fetching_call(
        taps_kernel,
        (jax.ShapeDtypeStruct(shape, jnp.bfloat16),) * 2,
        [pltpu.VMEM(shape, jnp.float32)] * 2,
        (),
        (),
        (conv_weight,),
    )


def chunk_call(members, tiles, *arrays):
    shape = tiles[0].shape
    return fetching_call(chunk_kernel, (f32((members, 2, 3) + shape), f32(shape)), [], (), tiles, arrays, GRANT)


def last_call(part, ahead_1, ahead_2, terms, recv, near_weight, far_weight):
    own, features = near_weight.shape
    (out,) = fetching_call(
        last_kernel,
        (jax.ShapeDtypeStruct((2 * part.shape[2], features // 2), jnp.bfloat16),),
        [
            pltpu.VMEM((2, 2 * own, features // 2), jnp.float32),
            pltpu.VMEM((LANES, features), jnp.float32),
        ],
        (),
        (part, ahead_1, ahead_2, terms, recv),
        (near_weight, far_weight),
    )
    return out


def forward_call(total_rows, rows, scalars, terms, bias_here, conv_bias, taps):
    own, width = bias_here.shape
    chans = 2 * own
    return call(
        functools.partial(forward_kernel, total_rows),
        (f32((rows, own, width)), f32((rows, own, width)), f32((rows + HALO, chans, width))),
        [
            pltpu.VMEM((rows + 2 * HALO, chans, width), jnp.float32),
            pltpu.VMEM((rows + 2 * HALO, chans, width), jnp.bfloat16),
            pltpu.VMEM((rows + HALO, chans, width), jnp.bfloat16),
            pltpu.VMEM((rows + HALO, own, width), jnp.float32),
            pltpu.VMEM((width + LANES, LANES), jnp.float32),
            pltpu.VMEM((LANES, LANES), jnp.float32),
            pltpu.VMEM((chans, width + LANES), jnp.float32),
            pltpu.VMEM((chans, LANES), jnp.float32),
            pltpu.VMEM((chans, width), jnp.float32),
            pltpu.VMEM(conv_bias.shape, conv_bias.dtype),
            pltpu.VMEM(terms.shape, terms.dtype),
            pltpu.VMEM(taps.shape, taps.dtype),
            pltpu.SemaphoreType.DMA((4,)),
        ],
        2 * 15 * chans * chans * width * 40,
        scalars,
        (),
        (terms,),
        (conv_bias, bias_here, taps),
    )


def backward_call(total_rows, members, scalars, cot_behind, cot, cot_ahead, slope_0, slope_1, last_slab, taps):
    rows, chans, width = cot.shape
    own = chans // 2
    slots = members + (width + LANES) // rows
    (terms,) = call(
        functools.partial(backward_kernel, total_rows),
        (jax.ShapeDtypeStruct((members, 2, rows, LANES), jnp.bfloat16),),
        [
            pltpu.VMEM((rows + 2 * HALO, chans, width), jnp.bfloat16),
            pltpu.VMEM((rows + HALO, own, width), jnp.float32),
            pltpu.VMEM((rows + HALO, chans, width), jnp.bfloat16),
            pltpu.VMEM((LANES, LANES), jnp.float32),
            pltpu.VMEM((LANES, width + LANES), jnp.float32),
            pltpu.VMEM((slots * rows, LANES), jnp.float32),
            pltpu.VMEM(taps.shape, taps.dtype),
            pltpu.VMEM(last_slab.shape, last_slab.dtype),
            pltpu.SemaphoreType.DMA((5,)),
        ],
        2 * 15 * chans * chans * width * 40,
        scalars,
        (slope_0, slope_1),
        (cot_behind, cot, cot_ahead, last_slab),
        (taps,),
    )
    return terms


def exchange_in_group(chunks):
    members = chunks.shape[0]
    lists = [
        [2 * (q * members + k) + c for k in range(members) for c in range(2)]
        for q in range(lax.axis_size("chrom") // members)
    ]
    flat = chunks.reshape((2 * members,) + chunks.shape[2:])
    recv = lax.all_to_all(flat, ("chrom", "chan"), 0, 0, axis_index_groups=lists)
    return recv.reshape(chunks.shape)


def from_edges(block, members):
    count = lax.axis_size("chrom")
    route = [(i + 3 * members, i) for i in range(0, count - 3 * members, members)]
    route += [(i - members, i) for i in range(2 * members - 1, count, members)]
    return lax.ppermute(block, "chrom", route)


def shards(
    embedding, window_start, band_width, dilations, near_weight, far_weight,
    distance_bias, conv_weight, conv_bias, cotangent,
):
    rows = embedding.shape[0]
    own, width = distance_bias.shape
    chans = conv_weight.shape[2]
    features_half = embedding.shape[1] // 2
    chan = lax.axis_index("chan")
    place = lax.axis_index("chrom")
    first_row = place * rows
    total_rows = lax.axis_size("chrom") * rows
    members = width // rows // 2
    member = place % members
    row_ids = first_row + jnp.arange(rows, dtype=jnp.int32)
    scalars = (dilations, band_width)

    near_weight, far_weight = near_weight.T, far_weight.T
    staged = jnp.swapaxes(cotangent, 0, 1)
    tile = tile_call((window_start,), after(embedding, staged), near_weight, far_weight)
    ahead = from_ahead(tile, members), from_ahead(tile, 2 * members), from_edges(tile, members)

    chunks, last_slab = chunk_call(
        members, (tile,) + ahead, conv_bias, distance_bias, near_weight, far_weight
    )
    terms = exchange_in_group(chunks)

    cot_other = from_partner(staged)
    offsets = jnp.arange(width, dtype=jnp.int32)
    keep = (offsets[None, :] < band_width[0]) & (row_ids[:, None] + offsets[None, :] < total_rows)
    cot = jnp.concatenate((staged, after(cot_other, chunks)), axis=1)
    cot = jnp.where(keep[:, None, :], cot, 0).astype(jnp.bfloat16)
    cot_behind = from_ahead(cot, -1)
    cot_ahead = from_ahead(cot, 1)

    taps_ahead, taps_back = taps_call(after(conv_weight, chunks))
    pair_rows, slope_0, slope_1 = forward_call(
        total_rows, rows, scalars, terms, distance_bias, conv_bias, taps_ahead
    )
    pair_out = jnp.swapaxes(pair_rows.astype(jnp.bfloat16), 0, 1)
    terms_back = backward_call(
        total_rows, members, scalars, cot_behind, cot, cot_ahead, slope_0, slope_1, last_slab, taps_back
    )
    recv = exchange_in_group(terms_back)
    part = jnp.sum(recv.astype(jnp.float32), axis=0).reshape(2, 2, rows // 2, LANES)
    ahead_1 = from_ahead(part[:, 0], -members)
    ahead_2 = from_ahead(part[:, 1], -2 * members)
    grads = last_call(part, ahead_1, ahead_2, terms, recv, near_weight, far_weight)
    return (pair_out, grads)


def solution(mesh):
    in_specs = (
        P("chrom", None),
        P(),
        P(),
        P(),
        P(None, "chan"),
        P(None, "chan"),
        P("chan", None),
        P(),
        P(None, "chan"),
        P("chan", "chrom", None),
    )
    out_specs = (P("chan", "chrom", None), P("chrom", "chan"))
    return jax.shard_map(shards, mesh=mesh, in_specs=in_specs, out_specs=out_specs, check_vma=False)
```
